512 devices in a mesh: depth: 8 (over y), plane: 64 (over x, z, core).
Axes of the slice: x: 4, y: 8, z: 8, core: 2. Of those that a mesh axis runs over, the one named last changes fastest.
Arguments:
- populations: float32 [8, 256, 19, 4096], P('depth', 'plane'), may hold values from 0.5 to 1.5
- fluid_mask: int32 [8, 256, 4096], P('depth', 'plane'), may hold values 0 or 1
- block_per_slot: int32 [256], replicated, may hold values from 0 to 128, as said below
- neighbours: int32 [128, 4], replicated, may hold values from 0 to 127, as said below
Outputs:
- evolved: float32 [8, 256, 19, 4096], P('depth', 'plane')
The draws below stay inside these ranges and needn't reach their ends.
Inputs may be any that keep to these rules, and one draw needn't show every extreme that they name: `block_per_slot`: each of the 128 blocks stands in exactly one slot; slots p * 4 to p * 4 + 3 belong to device p of the layer, its blocks first and then empty slots holding 128; every device holds 1 to 4 blocks and some device exactly 4. `neighbours`: the blocks form a periodic grid of 16 by 8; each row names the four blocks beside it in that grid.
All inputs are finite; a program needn't handle non-finite values. No bound on the sum of `fluid_mask` on one device may be relied on, other than what follows from the above.
Results may differ from the reference program's by a relative error of at most 0.0003.
Values sent between devices are 32-bit elements; how exact they have to be, the bound alone decides.
A program may use at most 128 MiB of HBM per device.

```python
import jax
import jax.numpy as jnp
import numpy as np
from jax import lax

BE = 16
CELLS = 4096
Q = 19
BLK_MEAN = 2
CAP = 4
GX = 16
STEPS = 2
NBL = 128
NS = 256
N_DEPTH = 8
N_PLANE = 64


def block_order(key):
    return jax.random.permutation(jax.random.fold_in(key, 101), NBL).astype(jnp.int32)


def draw_neighbours(key, part):
    ids_at_pos = block_order(key)
    rows_y = NBL // GX
    position = jnp.zeros((NBL,), jnp.int32).at[ids_at_pos].set(jnp.arange(NBL, dtype=jnp.int32))
    col_x = position // rows_y
    col_y = position % rows_y

    def block_at(index_x, index_y):
        return ids_at_pos[index_x % GX * rows_y + index_y % rows_y]
    return jnp.stack([block_at(col_x - 1, col_y), block_at(col_x + 1, col_y), block_at(col_x, col_y - 1), block_at(col_x, col_y + 1)], axis=1).astype(jnp.int32)


def draw_block_per_slot(key, part):
    ids_at_pos = block_order(key)
    key = jax.random.fold_in(key, 5)
    key_one, key_two = jax.random.split(key)
    dev_order = jax.random.permutation(key_one, N_PLANE).astype(jnp.int32)
    shifts = jax.random.randint(key_two, (N_PLANE,), -1, 2).astype(jnp.int32)
    ranks = jnp.arange(N_PLANE, dtype=jnp.int32)
    first = BLK_MEAN + 1
    offset_rank = ranks - first
    pair_index = jnp.maximum(offset_rank, 0) // 2
    partner = (pair_index * 2 + 1 < N_PLANE - first).astype(jnp.int32)
    signed = jnp.where(offset_rank % 2 == 0, shifts[pair_index], -shifts[pair_index]) * partner
    counts_rank = jnp.where(ranks == 0, CAP, jnp.where(ranks <= BLK_MEAN, BLK_MEAN - 1, BLK_MEAN + signed)).astype(jnp.int32)
    counts_run = counts_rank[dev_order]
    starts_run = jnp.cumsum(counts_run) - counts_run
    half_axis = N_PLANE // 2
    device_of_run = (ranks // 2 + ranks % 2 * half_axis).astype(jnp.int32)
    counts = jnp.zeros((N_PLANE,), jnp.int32).at[device_of_run].set(counts_run)
    starts = jnp.zeros((N_PLANE,), jnp.int32).at[device_of_run].set(starts_run.astype(jnp.int32))
    slot_dev = jnp.arange(NS, dtype=jnp.int32) // CAP
    slot_pos = jnp.arange(NS, dtype=jnp.int32) % CAP
    order = starts[slot_dev] + slot_pos
    return jnp.where(slot_pos < counts[slot_dev], ids_at_pos[jnp.minimum(order, NBL - 1)], NBL).astype(jnp.int32)


def place_ends(values, rng, smallest, largest):
    longest = values.shape.index(max(values.shape))
    spots = []
    for shift in (0, 1):
        where = [jax.random.randint(jax.random.fold_in(rng, axis), (), 0, length) for axis, length in enumerate(values.shape)]
        where[longest] = (where[longest] + shift) % values.shape[longest]
        spots.append(tuple(where))
    return values.at[spots[0]].set(smallest).at[spots[1]].set(largest)


def levels(key, extent, cuts, least, largest):
    gain, own = 1.0, jax.random.fold_in(key, 6)
    for dim, blocks in cuts:
        heights = jnp.exp(jax.random.uniform(jax.random.fold_in(own, dim), (blocks,), jnp.float32, least / len(cuts), largest / len(cuts)))
        gain = gain * jnp.repeat(heights, extent[dim] // blocks).reshape([-1 if axis == dim else 1 for axis in range(len(extent))])
    return gain


def setup_inputs(seed: int = 0) -> dict:
    seeds = jax.random.split(jax.random.key(seed), 5)
    populations = jnp.clip(0.5 + 1.0 * jax.random.uniform(seeds[0], (N_DEPTH, NS, Q, CELLS), jnp.float32) ** levels(seeds[0], (N_DEPTH, NS, Q, CELLS), ((0, 8), (1, 64)), -0.2, 0.2), 0.5, 1.5)
    fluid_mask = place_ends((jax.random.randint(seeds[1], (N_DEPTH, NS, CELLS), 0, 5) < 2).astype(jnp.int32), jax.random.fold_in(seeds[1], 1), 0, 1)
    block_per_slot = draw_block_per_slot(jax.random.fold_in(seeds[4], 71), 0)
    neighbours = draw_neighbours(jax.random.fold_in(seeds[4], 71), 0)
    return dict(populations=populations, fluid_mask=fluid_mask, block_per_slot=block_per_slot, neighbours=neighbours)


lattice_dirs = [(0, 0, 0), (1, 0, 0), (-1, 0, 0), (0, 1, 0), (0, -1, 0), (0, 0, 1), (0, 0, -1), (1, 1, 0), (-1, -1, 0), (1, -1, 0), (-1, 1, 0), (1, 0, 1), (-1, 0, -1), (1, 0, -1), (-1, 0, 1), (0, 1, 1), (0, -1, -1), (0, 1, -1), (0, -1, 1)]
opposite_dirs = [0, 2, 1, 4, 3, 6, 5, 8, 7, 10, 9, 12, 11, 14, 13, 16, 15, 18, 17]
xplus_dirs = [1, 7, 9, 11, 13]
xminus_dirs = [2, 8, 10, 12, 14]
positive_y_directions = [3, 7, 10, 15, 17]
yminus_dirs = [4, 8, 9, 16, 18]
zplus_dirs = [5, 11, 14, 15, 18]
zminus_dirs = [6, 12, 13, 16, 17]
relax_rates = [0.0, 1.19, 1.4, 0.0, 1.2, 0.0, 1.2, 0.0, 1.2, 1.25, 1.4, 1.25, 1.4, 1.25, 1.25, 1.25, 1.98, 1.98, 1.98]
table_order = (0, 1, 2, 3, 0, 1, 0, 1)


def weight_column():
    values = [1.0 / 3.0] + [1.0 / 18.0] * 6 + [1.0 / 36.0] * 12
    return jnp.asarray(np.array(values), jnp.float32)[:, None]


def moment_tables():
    velo = np.array(lattice_dirs) * 1.0
    cxv, cyv, czv = velo[:, 0], velo[:, 1], velo[:, 2]
    csq = cxv * cxv + cyv * cyv + czv * czv
    rows = [np.ones(19), 19.0 * csq - 30.0, (21.0 * csq * csq - 53.0 * csq + 24.0) / 2.0,
            cxv, (5.0 * csq - 9.0) * cxv, cyv, (5.0 * csq - 9.0) * cyv, czv, (5.0 * csq - 9.0) * czv,
            3.0 * cxv * cxv - csq, (3.0 * csq - 5.0) * (3.0 * cxv * cxv - csq),
            cyv * cyv - czv * czv, (3.0 * csq - 5.0) * (cyv * cyv - czv * czv),
            cxv * cyv, cyv * czv, cxv * czv,
            (cyv * cyv - czv * czv) * cxv, (czv * czv - cxv * cxv) * cyv, (cxv * cxv - cyv * cyv) * czv]
    matrix = np.stack(rows)
    inverse = matrix.T / np.sum(matrix * matrix, axis=1)[None, :]
    relax = inverse * np.array(relax_rates)[None, :]
    return jnp.asarray(matrix, jnp.float32), jnp.asarray(relax, jnp.float32)


def collide(population_field, fluid):
    matrix, relax = moment_tables()
    moments = jnp.einsum('qi,sic->sqc', matrix, population_field, precision=lax.Precision.HIGHEST)
    rho = moments[:, 0]
    jxv = moments[:, 3]
    jyv = moments[:, 5]
    jzv = moments[:, 7]
    jsq = jxv * jxv + jyv * jyv + jzv * jzv
    pxx = 2.0 * jxv * jxv - jyv * jyv - jzv * jzv
    pww = jyv * jyv - jzv * jzv
    empty_population = jnp.zeros_like(rho)
    equilibrium = jnp.stack([rho, -11.0 * rho + 19.0 * jsq, 3.0 * rho - 5.5 * jsq,
                             jxv, -2.0 / 3.0 * jxv, jyv, -2.0 / 3.0 * jyv, jzv, -2.0 / 3.0 * jzv,
                             pxx, -0.5 * pxx, pww, -0.5 * pww, jxv * jyv, jyv * jzv, jxv * jzv,
                             empty_population, empty_population, empty_population], axis=1)
    relaxed = population_field - jnp.einsum('qi,sic->sqc', relax, moments - equilibrium, precision=lax.Precision.HIGHEST)
    bounced = population_field[:, np.array(opposite_dirs), :]
    return jnp.where(fluid[:, None, :] == 1, relaxed, bounced)


def rims(post):
    slots = post.shape[0]
    cells = post.reshape(slots, 19, BE, BE, BE)
    top_layer = cells[:, np.array(zplus_dirs)][..., BE - 1].reshape(slots, 5, BE * BE)
    bottom_layer = cells[:, np.array(zminus_dirs)][..., 0].reshape(slots, 5, BE * BE)
    return top_layer, bottom_layer


def extend_depth(post, lower_rim, upper_rim):
    slots = post.shape[0]
    cells = post.reshape(slots, 19, BE, BE, BE)
    lower = jnp.zeros((slots, 19, BE, BE), jnp.float32).at[:, np.array(zplus_dirs)].set(lower_rim.reshape(slots, 5, BE, BE))
    upper = jnp.zeros((slots, 19, BE, BE), jnp.float32).at[:, np.array(zminus_dirs)].set(upper_rim.reshape(slots, 5, BE, BE))
    return jnp.concatenate([lower[..., None], cells, upper[..., None]], axis=-1)


def faces(padded):
    slots = padded.shape[0]
    width = BE * (BE + 2)
    xplus = padded[:, np.array(xplus_dirs)][:, :, BE - 1].reshape(slots, 5, width)
    xminus = padded[:, np.array(xminus_dirs)][:, :, 0].reshape(slots, 5, width)
    yplus = padded[:, np.array(positive_y_directions)][:, :, :, BE - 1].reshape(slots, 5, width)
    yminus = padded[:, np.array(yminus_dirs)][:, :, :, 0].reshape(slots, 5, width)
    return xplus, xminus, yplus, yminus


def source_slots(my_blocks, block_per_slot, neighbours):
    block_total = neighbours.shape[0]
    slot_total = block_per_slot.shape[0]
    slot_lookup = jnp.zeros((block_total,), jnp.int32).at[block_per_slot].set(jnp.arange(slot_total, dtype=jnp.int32), mode="drop")
    blocks = jnp.minimum(my_blocks, block_total - 1)
    near = neighbours[blocks]
    return jnp.stack([slot_lookup[near[:, 0]], slot_lookup[near[:, 1]], slot_lookup[near[:, 2]], slot_lookup[near[:, 3]],
                      slot_lookup[neighbours[near[:, 0], 2]], slot_lookup[neighbours[near[:, 1], 3]],
                      slot_lookup[neighbours[near[:, 0], 3]], slot_lookup[neighbours[near[:, 1], 2]]], axis=0)


def gather_layers(block_z, xp_in, xm_in, yp_in, ym_in, corner_a, corner_b, corner_c, corner_d):
    ext = jnp.pad(block_z, ((0, 0), (1, 1), (1, 1), (0, 0)))
    ext = ext.at[np.array(xplus_dirs), 0, 1:BE + 1, :].set(xp_in)
    ext = ext.at[np.array(xminus_dirs), BE + 1, 1:BE + 1, :].set(xm_in)
    ext = ext.at[np.array(positive_y_directions), 1:BE + 1, 0, :].set(yp_in)
    ext = ext.at[np.array(yminus_dirs), 1:BE + 1, BE + 1, :].set(ym_in)
    ext = ext.at[7, 0, 0, :].set(corner_a)
    ext = ext.at[8, BE + 1, BE + 1, :].set(corner_b)
    ext = ext.at[9, 0, BE + 1, :].set(corner_c)
    ext = ext.at[10, BE + 1, 0, :].set(corner_d)
    pieces = []
    for which in range(19):
        cxv, cyv, czv = lattice_dirs[which]
        pieces.append(ext[which, 1 - cxv:1 - cxv + BE, 1 - cyv:1 - cyv + BE, 1 - czv:1 - czv + BE])
    return jnp.stack(pieces).reshape(19, BE * BE * BE)


def finish(padded, picked):
    slots = padded.shape[0]
    shaped = [piece.reshape(slots, 5, BE, BE + 2) for piece in picked]
    corner_a = shaped[4][:, 1, BE - 1, :]
    corner_b = shaped[5][:, 1, 0, :]
    corner_c = shaped[6][:, 2, 0, :]
    corner_d = shaped[7][:, 2, BE - 1, :]
    return jax.vmap(gather_layers)(padded, shaped[0], shaped[1], shaped[2], shaped[3], corner_a, corner_b, corner_c, corner_d)


def layer_stream(post, lower_rim, upper_rim, block_per_slot, neighbours):
    padded = extend_depth(post, lower_rim, upper_rim)
    tables = faces(padded)
    sources = source_slots(block_per_slot, block_per_slot, neighbours)
    picked = [jnp.take(tables[table_order[which]], sources[which], axis=0) for which in range(8)]
    return finish(padded, picked)


def reference(populations, fluid_mask, block_per_slot, neighbours):
    column = weight_column()
    population_field = populations * column
    valid = block_per_slot < neighbours.shape[0]
    for repeat in range(STEPS):
        post = lax.map(lambda items: collide(items[0], items[1]), (population_field, fluid_mask))
        top_layer, bottom_layer = jax.vmap(rims)(post)
        lower_rim = jnp.roll(top_layer, 1, axis=0)
        upper_rim = jnp.roll(bottom_layer, -1, axis=0)
        population_field = lax.map(lambda items: layer_stream(items[0], items[1], items[2], block_per_slot, neighbours), (post, lower_rim, upper_rim))
    population_field = jnp.where(valid[None, :, None, None], population_field, 0.0)
    return population_field / column
```

```python
import functools

import jax
import jax.numpy as jnp
from jax import lax
from jax.experimental import pallas as pl
from jax.experimental.pallas import tpu as pltpu
from jax.sharding import PartitionSpec as P

MESH = pl.DeviceIdType.MESH
BE = 16
CAP = 4
STEPS = 2
Q = 19
F32 = jnp.float32
PLANE_DIMS = {64: (4, 8, 2)}

DIRS = [
    (0, 0, 0),
    (1, 0, 0),
    (-1, 0, 0),
    (0, 1, 0),
    (0, -1, 0),
    (0, 0, 1),
    (0, 0, -1),
    (1, 1, 0),
    (-1, -1, 0),
    (1, -1, 0),
    (-1, 1, 0),
    (1, 0, 1),
    (-1, 0, -1),
    (1, 0, -1),
    (-1, 0, 1),
    (0, 1, 1),
    (0, -1, -1),
    (0, 1, -1),
    (0, -1, 1),
]
OPP = [0, 2, 1, 4, 3, 6, 5, 8, 7, 10, 9, 12, 11, 14, 13, 16, 15, 18, 17]
WEIGHTS = [1.0 / 3.0] + [1.0 / 18.0] * 6 + [1.0 / 36.0] * 12
ZPLUS = [5, 11, 14, 15, 18]
ZMINUS = [6, 12, 13, 16, 17]
OFF = [1 if d[1] > 0 else 0 for d in DIRS]
HALO = [0 if d[1] > 0 else 2 for d in DIRS]
MAIN = slice(8, 24)
LOW, HIGH = slice(7, 8), slice(24, 25)
FIRST, LAST = slice(8, 9), slice(23, 24)


def sources_kernel(slots_ref, near_ref, out_ref):
    blocks, slots = near_ref.shape[0], slots_ref.shape[1]
    held = slots_ref[...]
    onehot = lax.broadcasted_iota(jnp.int32, (blocks, slots), 0) == held
    number = lax.broadcasted_iota(jnp.int32, (blocks, slots), 1).astype(F32)
    lookup = jnp.sum(jnp.where(onehot, number, 0.0), axis=1, keepdims=True)
    lane = lax.broadcasted_iota(jnp.int32, (blocks, blocks), 1)
    hops = [(near_ref[:, k : k + 1] == lane).astype(F32) for k in range(4)]

    def through(k, column):
        wide = jnp.broadcast_to(column, (blocks, 128))
        return jnp.dot(
            hops[k], wide, preferred_element_type=F32, precision=lax.Precision.HIGHEST
        )[:, :1]

    one = [through(k, lookup) for k in range(4)]
    two = [through(0, one[2]), through(1, one[3]), through(0, one[3]), through(1, one[2])]
    place = lax.broadcasted_iota(jnp.int32, (blocks, 8), 1)
    table = jnp.zeros((blocks, 8), F32)
    for k, column in enumerate(one + two):
        table = jnp.where(place == k, column, table)
    found = lax.dot_general(
        table,
        onehot.astype(F32),
        (((0,), (0,)), ((), ())),
        preferred_element_type=F32,
        precision=lax.Precision.HIGHEST,
    )
    out_ref[0:8, :] = (found + 0.5).astype(jnp.int32)
    out_ref[8:16, :] = jnp.broadcast_to((held < blocks).astype(jnp.int32), (8, slots))


def collided(f, fluid):
    s1, d1 = f[1] + f[2], f[1] - f[2]
    s2, d2 = f[3] + f[4], f[3] - f[4]
    s3, d3 = f[5] + f[6], f[5] - f[6]
    a, da = f[7] + f[8], f[7] - f[8]
    b, db = f[9] + f[10], f[9] - f[10]
    c, dc = f[11] + f[12], f[11] - f[12]
    d, dd = f[13] + f[14], f[13] - f[14]
    e, de = f[15] + f[16], f[15] - f[16]
    g, dg = f[17] + f[18], f[17] - f[18]
    sxy, sxz, syz = a + b, c + d, e + g
    x_xy, y_xy = da + db, da - db
    x_xz, z_xz = dc + dd, dc - dd
    y_yz, z_yz = de + dg, de - dg
    axis = s1 + s2 + s3
    diag = sxy + sxz + syz
    xx, yy, zz = x_xy + x_xz, y_xy + y_yz, z_xz + z_yz
    rho = f[0] + axis + diag
    jx, jy, jz = d1 + xx, d2 + yy, d3 + zz
    jx2, jy2, jz2 = jx * jx, jy * jy, jz * jz
    jsq = jx2 + jy2 + jz2
    pxx_eq = 2.0 * jx2 - jy2 - jz2
    pww_eq = jy2 - jz2
    m_e = 8.0 * diag - 11.0 * axis - 30.0 * f[0]
    m_eps = diag - 4.0 * axis + 12.0 * f[0]
    yz_axis = s2 + s3
    part = sxy + sxz - 2.0 * syz
    split = sxy - sxz
    turn = s2 - s3
    k_e = (1.19 / 2394.0) * (m_e + 11.0 * rho - 19.0 * jsq)
    k_eps = (1.4 / 252.0) * (m_eps - 3.0 * rho + 5.5 * jsq)
    k_qx = (1.2 / 40.0) * (xx - 4.0 * d1 + (2.0 / 3.0) * jx)
    k_qy = (1.2 / 40.0) * (yy - 4.0 * d2 + (2.0 / 3.0) * jy)
    k_qz = (1.2 / 40.0) * (zz - 4.0 * d3 + (2.0 / 3.0) * jz)
    k_pxx = (1.25 / 36.0) * (2.0 * s1 - yz_axis + part - pxx_eq)
    k_pixx = (1.4 / 72.0) * (2.0 * yz_axis - 4.0 * s1 + part + 0.5 * pxx_eq)
    k_pww = (1.25 / 12.0) * (turn + split - pww_eq)
    k_piww = (1.4 / 24.0) * (split - 2.0 * turn + 0.5 * pww_eq)
    k_pxy = (1.25 / 4.0) * (a - b - jx * jy)
    k_pyz = (1.25 / 4.0) * (e - g - jy * jz)
    k_pxz = (1.25 / 4.0) * (c - d - jx * jz)
    k_mx = (1.98 / 8.0) * (x_xy - x_xz)
    k_my = (1.98 / 8.0) * (y_yz - y_xy)
    k_mz = (1.98 / 8.0) * (z_xz - z_yz)
    axial = 11.0 * k_e + 4.0 * k_eps
    sides = k_pxx - 2.0 * k_pixx
    tilt = k_pww - 2.0 * k_piww
    ax = 2.0 * sides - axial
    ay = tilt - sides - axial
    az = -tilt - sides - axial
    even = 8.0 * k_e + k_eps
    both = k_pxx + k_pixx
    lean = k_pww + k_piww
    exy = even + both + lean
    exz = even + both - lean
    eyz = even - 2.0 * both
    ux, uy, uz = 4.0 * k_qx, 4.0 * k_qy, 4.0 * k_qz
    xy_x, xy_y = k_qx + k_mx, k_qy - k_my
    xz_x, xz_z = k_qx - k_mx, k_qz + k_mz
    yz_y, yz_z = k_qy + k_my, k_qz - k_mz
    p, m = exy + k_pxy, exy - k_pxy
    add, sub = xy_x + xy_y, xy_x - xy_y
    change = [12.0 * k_eps - 30.0 * k_e, ax - ux, ax + ux, ay - uy, ay + uy, az - uz, az + uz]
    change += [p + add, p - add, m + sub, m - sub]
    p, m = exz + k_pxz, exz - k_pxz
    add, sub = xz_x + xz_z, xz_x - xz_z
    change += [p + add, p - add, m + sub, m - sub]
    p, m = eyz + k_pyz, eyz - k_pyz
    add, sub = yz_y + yz_z, yz_y - yz_z
    change += [p + add, p - add, m + sub, m - sub]
    return [jnp.where(fluid, f[i] - change[i], f[OPP[i]]) for i in range(Q)]


def skewed(rows, base, stride):
    return pltpu.roll(rows, base, 1, stride=stride, stride_axis=0)


def spread(rows, turns):
    for t in turns:
        rows = rows + pltpu.roll(rows, t, 1)
    return rows


def kernel(dims, near_ref, pop_ref, mask_ref, out_ref, tiles, field, fluid, ext, *rest):
    nx, nz, nc = dims
    nd = lax.axis_size("depth")
    per_x = nz * nc * CAP
    layer = lax.axis_index("depth")
    me = lax.axis_index("plane")
    core = me % nc
    z = (me // nc) % nz
    x = me // (nc * nz)
    turn = 1 - 2 * core
    mine = (z * nc + core) * CAP
    first_slot = me * CAP

    def plane(xx, zz, cc):
        return {"plane": (xx * nz + zz) * nc + cc}

    above = {"depth": (layer + 1) % nd}
    below = {"depth": (layer + nd - 1) % nd}
    ring_a = plane(x, (z + turn + nz) % nz, core)
    ring_b = plane(x, (z - turn + nz) % nz, core)
    twin = plane(x, z, 1 - core)
    across = [plane((x + k) % nx, z, core) for k in range(1, nx)]

    barrier = pltpu.get_barrier_semaphore()
    partners = [above, below, ring_a, ring_b, twin] + across
    for other in partners:
        pl.semaphore_signal(barrier, inc=1, device_id=other, device_id_type=MESH)

    send_sems, recv_sems = rest[-2:]
    per_step = rest[:-2]
    used = [0]

    def copy(src, dst, device):
        n = used[0]
        used[0] += 1
        return pltpu.make_async_remote_copy(
            src_ref=src,
            dst_ref=dst,
            send_sem=send_sems.at[n],
            recv_sem=recv_sems.at[n],
            device_id=device,
            device_id_type=MESH,
        )

    lane = lax.broadcasted_iota(jnp.int32, (BE, 128), 1)
    row = lax.broadcasted_iota(jnp.int32, (BE, 128), 0)
    zin = lane % BE
    low_lanes, high_lanes = lane < BE, lane >= 128 - BE
    own_row = zin == row
    own_group = lane // BE == row % 8
    tile_row = lax.broadcasted_iota(jnp.int32, (8, 128), 0)

    for t in range(32):
        tiles[0, 8 * t : 8 * t + CAP, :] = mask_ref[0, :, 128 * t : 128 * t + 128].astype(F32)
    for s in range(CAP):
        for h in range(2):
            fluid[s, h] = tiles[0, pl.ds(8 * h + s, BE, stride=16), :]

    def take_in(s, carry):
        for g in range(3):
            rows = min(8, Q - 8 * g)
            for t in range(32):
                tiles[g, 8 * t : 8 * t + rows, :] = pop_ref[
                    0, s, 8 * g : 8 * g + rows, 128 * t : 128 * t + 128
                ]
        for i in range(Q):
            for h in range(2):
                part = tiles[i // 8, pl.ds(8 * h + i % 8, BE, stride=16), :]
                field[s, i, h] = part * WEIGHTS[i]
        return carry

    lax.fori_loop(0, CAP, take_in, 0)

    def collide_all(up, down):
        def body(n, carry):
            s, h = n // 2, n % 2
            f = [field[s, i, h] for i in range(Q)]
            post = collided(f, fluid[s, h] == 1.0)
            for i in range(Q):
                ext[s, i, h + OFF[i], MAIN, :] = post[i]
            for k, i in enumerate(ZPLUS):
                packed = jnp.where(own_row, skewed(post[i], 1, 1), 0.0)
                up[pl.ds(s * 10 + k * 2 + h, 1), :] = jnp.sum(packed, axis=0, keepdims=True)
            for k, i in enumerate(ZMINUS):
                packed = jnp.where(own_row, skewed(post[i], 0, 1), 0.0)
                down[pl.ds(s * 10 + k * 2 + h, 1), :] = jnp.sum(packed, axis=0, keepdims=True)
            return carry

        lax.fori_loop(0, 2 * CAP, body, 0)

    def put_y(table, s, tile, start, i):
        if DIRS[i][1] > 0:
            moved = skewed(ext[s, i, 2, MAIN, :], BE, BE)
        else:
            moved = skewed(ext[s, i, 0, MAIN, :], 0, BE)
        kept = jnp.where(own_group, moved, 0.0)
        for q in range(2):
            table[mine + s, tile, start + q : start + q + 1, :] = jnp.sum(
                kept[8 * q : 8 * q + 8], axis=0, keepdims=True
            )

    def put_x(table, s, tile, start, i):
        edge = LAST if DIRS[i][0] > 0 else FIRST
        for h in range(2):
            table[mine + s, tile, start + h : start + h + 1, :] = ext[s, i, h + OFF[i], edge, :]

    def pack_early(table):
        def body(s, carry):
            for k, i in enumerate((1, 7, 9)):
                put_x(table, s, 0, 2 * k, i)
            table[mine + s, 0, 6:7, :] = ext[s, 7, 2, LAST, :]
            table[mine + s, 0, 7:8, :] = ext[s, 9, 0, LAST, :]
            for k, i in enumerate((2, 8, 10)):
                put_x(table, s, 1, 2 * k, i)
            table[mine + s, 1, 6:7, :] = ext[s, 8, 0, FIRST, :]
            table[mine + s, 1, 7:8, :] = ext[s, 10, 2, FIRST, :]
            for k, i in enumerate((3, 7, 10)):
                put_y(table, s, 2, 2 * k, i)
                put_y(table, s, 3, 2 * k, OPP[i])
            for tile in (2, 3):
                table[mine + s, tile, 6:8, :] = jnp.zeros((2, 128), F32)
            return carry

        lax.fori_loop(0, CAP, body, 0)

    def shift_z(from_below, from_above, table):
        def body(s, carry):
            for k, i in enumerate(ZPLUS):
                for h in range(2):
                    rim = from_below[pl.ds(s * 10 + k * 2 + h, 1), :]
                    rim = jnp.broadcast_to(pltpu.roll(rim, 128 - BE, 1), (BE, 128))
                    rim = spread(jnp.where(own_row, rim, 0.0), (120, 124, 126, 127))
                    part = ext[s, i, h + OFF[i], MAIN, :]
                    ext[s, i, h + OFF[i], MAIN, :] = jnp.where(
                        zin == 0, rim, pltpu.roll(part, 1, 1)
                    )
            for k, i in enumerate(ZMINUS):
                for h in range(2):
                    rim = from_above[pl.ds(s * 10 + k * 2 + h, 1), :]
                    rim = jnp.broadcast_to(rim, (BE, 128))
                    rim = spread(jnp.where(own_row, rim, 0.0), (8, 4, 2, 1))
                    part = ext[s, i, h + OFF[i], MAIN, :]
                    ext[s, i, h + OFF[i], MAIN, :] = jnp.where(
                        zin == BE - 1, rim, pltpu.roll(part, 127, 1)
                    )
            for k, i in enumerate((11, 13, 12, 14)):
                put_x(table, s, 0, 2 * k, i)
            for k, i in enumerate((15, 17, 16, 18)):
                put_y(table, s, 1, 2 * k, i)
            return carry

        lax.fori_loop(0, CAP, body, 0)

    class Ring:
        def __init__(self, table):
            def block(zz):
                return table.at[pl.ds((((zz + 2 * nz) % nz) * nc + core) * CAP, CAP)]

            self.a = [
                copy(block(z - turn * t), block(z - turn * t), ring_a) for t in range(nz // 2)
            ]
            self.b = [
                copy(block(z + turn * t), block(z + turn * t), ring_b)
                for t in range((nz - 1) // 2)
            ]
            self.twin = [copy(block(z), block(z), twin)]
            self.twin += [
                copy(block(z - turn * t), block(z - turn * t), twin)
                for t in range(1, nz // 2 + 1)
            ]
            self.twin_b = len(self.twin)
            self.twin += [
                copy(block(z + turn * t), block(z + turn * t), twin)
                for t in range(1, (nz - 1) // 2 + 1)
            ]

        def begin(self):
            self.a[0].start()
            if self.b:
                self.b[0].start()
            self.twin[0].start()

        def hop(self, t):
            if t <= len(self.a):
                self.a[t - 1].wait_recv()
                if t < len(self.a):
                    self.a[t].start()
                self.twin[t].start()
            if t <= len(self.b):
                self.b[t - 1].wait_recv()
                if t < len(self.b):
                    self.b[t].start()
                self.twin[self.twin_b + t - 1].start()

        def end(self):
            for c in self.twin:
                c.wait_recv()

        def sent(self):
            for c in self.a + self.b + self.twin:
                c.wait_send()

    def source(k, xx, s):
        return near_ref[k, xx * per_x + mine + s]

    def early_row(table, to, base, xx):
        def body(s, carry):
            at = [source(k, xx, s) % per_x for k in range(8)]
            for tile, (main, six, seven) in enumerate(((0, 4, 6), (1, 5, 7))):
                got = jnp.where(tile_row == 6, table[at[six], tile], table[at[main], tile])
                to[base + s, tile] = jnp.where(tile_row == 7, table[at[seven], tile], got)
            to[base + s, 2] = table[at[2], 2]
            to[base + s, 3] = table[at[3], 3]
            return carry

        lax.fori_loop(0, CAP, body, 0)

    def late_row(table, to, base, xx):
        def body(s, carry):
            at = [source(k, xx, s) % per_x for k in range(4)]
            for tile in range(2):
                to[base + s, tile] = jnp.where(
                    tile_row < 4, table[at[2 * tile], tile], table[at[2 * tile + 1], tile]
                )
            return carry

        lax.fori_loop(0, CAP, body, 0)

    def hand_out(fill, table, out, got):
        sends = []
        for k in range(1, nx):
            fill(table, out, (k - 1) * CAP, (x + k) % nx)
            c = copy(
                out.at[pl.ds((k - 1) * CAP, CAP)], got.at[pl.ds(x * CAP, CAP)], across[k - 1]
            )
            c.start()
            sends.append(c)
        fill(table, got, x * CAP, x)
        return sends

    def take_y(s, i, two):
        wide = [jnp.broadcast_to(two[q : q + 1], (8, 128)) for q in range(2)]
        kept = jnp.where(own_group, jnp.concatenate(wide, axis=0), 0.0)
        ext[s, i, HALO[i], MAIN, :] = spread(kept, (64, 32, 16))

    def place_halos(early, late):
        def body(s, carry):
            of = [(source(k, x, s) // per_x) * CAP + s for k in range(8)]

            def put(i, h, value):
                ext[s, i, h, LOW if DIRS[i][0] > 0 else HIGH, :] = value

            for tile, faces in enumerate(((1, 7, 9), (2, 8, 10))):
                for k, i in enumerate(faces):
                    for h in range(2):
                        r = 2 * k + h
                        put(i, h + OFF[i], early[of[tile], tile, r : r + 1, :])
            put(7, 0, early[of[4], 0, 6:7, :])
            put(9, 2, early[of[6], 0, 7:8, :])
            put(8, 2, early[of[5], 1, 6:7, :])
            put(10, 0, early[of[7], 1, 7:8, :])
            for k, i in enumerate((3, 7, 10)):
                take_y(s, i, early[of[2], 2, 2 * k : 2 * k + 2, :])
                take_y(s, OPP[i], early[of[3], 3, 2 * k : 2 * k + 2, :])
            for k, i in enumerate((11, 13, 12, 14)):
                for h in range(2):
                    r = 2 * k + h
                    put(i, h, late[of[k // 2], 0, r : r + 1, :])
            for k, i in enumerate((15, 17, 16, 18)):
                take_y(s, i, late[of[2 + k // 2], 1, 2 * k : 2 * k + 2, :])
            return carry

        lax.fori_loop(0, CAP, body, 0)

    def shift_xy():
        def body(s, carry):
            for i in range(Q):
                cx, cy, _ = DIRS[i]
                rows = slice(8 - cx, 24 - cx)
                if cy == 0:
                    for h in range(2):
                        field[s, i, h] = ext[s, i, h, rows, :]
                    continue
                e = [ext[s, i, h, rows, :] for h in range(3)]
                for h in range(2):
                    if cy > 0:
                        field[s, i, h] = pltpu.roll(
                            jnp.where(high_lanes, e[h], e[h + 1]), BE, 1
                        )
                    else:
                        field[s, i, h] = pltpu.roll(
                            jnp.where(low_lanes, e[h + 1], e[h]), 128 - BE, 1
                        )
            return carry

        lax.fori_loop(0, CAP, body, 0)

    for step in range(STEPS):
        up, down, low, high, table_e, table_l, out_e, out_l, got_e, got_l = per_step[
            10 * step : 10 * step + 10
        ]
        collide_all(up, down)
        if step == 0:
            pl.semaphore_wait(barrier, len(partners))
        rims = [copy(up, low, above), copy(down, high, below)]
        for c in rims:
            c.start()
        pack_early(table_e)
        early = Ring(table_e)
        early.begin()
        for c in rims:
            c.wait_recv()
        shift_z(low, high, table_l)
        late = Ring(table_l)
        late.begin()
        hops = nz // 2
        early.hop(1)
        for t in range(2, hops + 1):
            early.hop(t)
            late.hop(t - 1)
        early.end()
        sends = hand_out(early_row, table_e, out_e, got_e)
        late.hop(hops)
        late.end()
        sends += hand_out(late_row, table_l, out_l, got_l)
        for c in sends:
            c.wait_recv()
        place_halos(got_e, got_l)
        shift_xy()
        early.sent()
        late.sent()
        for c in rims + sends:
            c.wait_send()

    def give_out(s, carry):
        held = near_ref[8, first_slot + s] == 1
        for i in range(Q):
            for h in range(2):
                part = jnp.where(held, field[s, i, h] * (1.0 / WEIGHTS[i]), 0.0)
                tiles[i // 8, pl.ds(8 * h + i % 8, BE, stride=16), :] = part
        for g in range(3):
            rows = min(8, Q - 8 * g)
            for t in range(32):
                out_ref[0, s, 8 * g : 8 * g + rows, 128 * t : 128 * t + 128] = tiles[
                    g, 8 * t : 8 * t + rows, :
                ]
        return carry

    lax.fori_loop(0, CAP, give_out, 0)


def solution(mesh):
    planes = mesh.shape["plane"]
    dims = PLANE_DIMS[planes]
    nx, nz, nc = dims
    group = nz * nc * CAP

    def shards(populations, fluid_mask, block_per_slot, neighbours):
        slots = block_per_slot.shape[0]
        near = pl.pallas_call(
            sources_kernel,
            out_shape=jax.ShapeDtypeStruct((16, slots), jnp.int32),
            in_specs=[pl.BlockSpec(memory_space=pltpu.VMEM)] * 2,
            out_specs=pl.BlockSpec(memory_space=pltpu.VMEM),
        )(block_per_slot.reshape(1, slots), neighbours)
        scratch = [
            pltpu.VMEM((3, 256, 128), F32),
            pltpu.VMEM((CAP, Q, 2, BE, 128), F32),
            pltpu.VMEM((CAP, 2, BE, 128), F32),
            pltpu.VMEM((CAP, Q, 3, 32, 128), F32),
        ]
        for _ in range(STEPS):
            scratch += [pltpu.VMEM((10 * CAP, 128), F32)] * 4
            for count, tiles in ((group, 4), (group, 2)):
                scratch.append(pltpu.VMEM((count, tiles, 8, 128), F32))
            for tiles in (4, 2):
                scratch.append(pltpu.VMEM(((nx - 1) * CAP, tiles, 8, 128), F32))
            for tiles in (4, 2):
                scratch.append(pltpu.VMEM((nx * CAP, tiles, 8, 128), F32))
        ring = nz // 2 + (nz - 1) // 2 + nz
        copies = STEPS * (2 + 2 * ring + 2 * (nx - 1))
        scratch += [pltpu.SemaphoreType.DMA((copies,)), pltpu.SemaphoreType.DMA((copies,))]
        vmem = pl.BlockSpec(memory_space=pltpu.VMEM)
        return pl.pallas_call(
            functools.partial(kernel, dims),
            out_shape=jax.ShapeDtypeStruct(populations.shape, F32),
            in_specs=[pl.BlockSpec(memory_space=pltpu.SMEM), vmem, vmem],
            out_specs=vmem,
            scratch_shapes=scratch,
            compiler_params=pltpu.CompilerParams(
                collective_id=0, has_side_effects=True, vmem_limit_bytes=40 * 1024 * 1024
            ),
        )(near, populations, fluid_mask)

    return jax.shard_map(
        shards,
        mesh=mesh,
        in_specs=(P("depth", "plane", None, None), P("depth", "plane", None), P(), P()),
        out_specs=P("depth", "plane", None, None),
        check_vma=False,
    )
```

```python
import functools

import jax
import jax.numpy as jnp
from jax import lax
from jax.experimental import pallas as pl
from jax.experimental.pallas import tpu as pltpu
from jax.sharding import PartitionSpec as P

MESH = pl.DeviceIdType.MESH
BE = 16
CAP = 4
STEPS = 2
Q = 19
F32 = jnp.float32
PLANE_DIMS = {64: (4, 8, 2)}

DIRS = [
    (0, 0, 0),
    (1, 0, 0),
    (-1, 0, 0),
    (0, 1, 0),
    (0, -1, 0),
    (0, 0, 1),
    (0, 0, -1),
    (1, 1, 0),
    (-1, -1, 0),
    (1, -1, 0),
    (-1, 1, 0),
    (1, 0, 1),
    (-1, 0, -1),
    (1, 0, -1),
    (-1, 0, 1),
    (0, 1, 1),
    (0, -1, -1),
    (0, 1, -1),
    (0, -1, 1),
]
OPP = [0, 2, 1, 4, 3, 6, 5, 8, 7, 10, 9, 12, 11, 14, 13, 16, 15, 18, 17]
WEIGHTS = [1.0 / 3.0] + [1.0 / 18.0] * 6 + [1.0 / 36.0] * 12
ZPLUS = [5, 11, 14, 15, 18]
ZMINUS = [6, 12, 13, 16, 17]
EARLY = ((1, 7, 9), (2, 8, 10), (3, 7, 10), (4, 8, 9))
LATE = ((11, 13, 12, 14), (15, 17, 16, 18))
YDIRS = [i for i in range(Q) if DIRS[i][1] != 0]


def top_rows(v):
    total = v[0:8]
    for r in range(8, v.shape[0], 8):
        total = jnp.maximum(total, v[r : r + 8])
    for t in (4, 2, 1):
        total = jnp.maximum(total, pltpu.roll(total, t, 0))
    return total


def find_sources(slots_ref, near_ref, out_ref):
    blocks, slots = near_ref.shape[1], slots_ref.shape[1]
    held = slots_ref[...]
    down = lax.broadcasted_iota(jnp.int32, (blocks, 128), 0)
    across = lax.broadcasted_iota(jnp.int32, (blocks, 128), 1)

    def upright(line):
        return jnp.transpose(jnp.broadcast_to(line, (128, 128)))

    lookup = jnp.zeros((8, 128), jnp.int32)
    for q in range(slots // 128):
        mine = upright(held[:, 128 * q : 128 * q + 128])
        lookup = jnp.maximum(lookup, top_rows(jnp.where(mine == across, down + 128 * q, 0)))

    def through(k, column):
        hit = jnp.broadcast_to(near_ref[k : k + 1, :], (blocks, 128)) == down
        return top_rows(jnp.where(hit, column, 0))[0:1]

    column = upright(lookup[0:1])
    found = [upright(through(k, column)) for k in range(4)]
    found += [upright(through(k, found[j])) for k, j in ((0, 2), (1, 3), (0, 3), (1, 2))]
    for q in range(slots // 128):
        part = slice(128 * q, 128 * q + 128)
        hit = jnp.broadcast_to(held[:, part], (blocks, 128)) == down
        for k in range(8):
            out_ref[k : k + 1, part] = top_rows(jnp.where(hit, found[k], 0))[0:1]
        out_ref[8:16, part] = jnp.broadcast_to(
            jnp.where(held[:, part] < blocks, 1, 0), (8, 128)
        )


def collided(f, fluid):
    s1, d1 = f[1] + f[2], f[1] - f[2]
    s2, d2 = f[3] + f[4], f[3] - f[4]
    s3, d3 = f[5] + f[6], f[5] - f[6]
    a, da = f[7] + f[8], f[7] - f[8]
    b, db = f[9] + f[10], f[9] - f[10]
    c, dc = f[11] + f[12], f[11] - f[12]
    d, dd = f[13] + f[14], f[13] - f[14]
    e, de = f[15] + f[16], f[15] - f[16]
    g, dg = f[17] + f[18], f[17] - f[18]
    sxy, sxz, syz = a + b, c + d, e + g
    x_xy, y_xy = da + db, da - db
    x_xz, z_xz = dc + dd, dc - dd
    y_yz, z_yz = de + dg, de - dg
    axis = s1 + s2 + s3
    diag = sxy + sxz + syz
    xx, yy, zz = x_xy + x_xz, y_xy + y_yz, z_xz + z_yz
    rho = f[0] + axis + diag
    jx, jy, jz = d1 + xx, d2 + yy, d3 + zz
    jx2, jy2, jz2 = jx * jx, jy * jy, jz * jz
    jsq = jx2 + jy2 + jz2
    pxx_eq = 2.0 * jx2 - jy2 - jz2
    pww_eq = jy2 - jz2
    m_e = 8.0 * diag - 11.0 * axis - 30.0 * f[0]
    m_eps = diag - 4.0 * axis + 12.0 * f[0]
    yz_axis = s2 + s3
    part = sxy + sxz - 2.0 * syz
    split = sxy - sxz
    turn = s2 - s3
    k_e = (1.19 / 2394.0) * (m_e + 11.0 * rho - 19.0 * jsq)
    k_eps = (1.4 / 252.0) * (m_eps - 3.0 * rho + 5.5 * jsq)
    k_qx = (1.2 / 40.0) * (xx - 4.0 * d1 + (2.0 / 3.0) * jx)
    k_qy = (1.2 / 40.0) * (yy - 4.0 * d2 + (2.0 / 3.0) * jy)
    k_qz = (1.2 / 40.0) * (zz - 4.0 * d3 + (2.0 / 3.0) * jz)
    k_pxx = (1.25 / 36.0) * (2.0 * s1 - yz_axis + part - pxx_eq)
    k_pixx = (1.4 / 72.0) * (2.0 * yz_axis - 4.0 * s1 + part + 0.5 * pxx_eq)
    k_pww = (1.25 / 12.0) * (turn + split - pww_eq)
    k_piww = (1.4 / 24.0) * (split - 2.0 * turn + 0.5 * pww_eq)
    k_pxy = (1.25 / 4.0) * (a - b - jx * jy)
    k_pyz = (1.25 / 4.0) * (e - g - jy * jz)
    k_pxz = (1.25 / 4.0) * (c - d - jx * jz)
    k_mx = (1.98 / 8.0) * (x_xy - x_xz)
    k_my = (1.98 / 8.0) * (y_yz - y_xy)
    k_mz = (1.98 / 8.0) * (z_xz - z_yz)
    axial = 11.0 * k_e + 4.0 * k_eps
    sides = k_pxx - 2.0 * k_pixx
    tilt = k_pww - 2.0 * k_piww
    ax = 2.0 * sides - axial
    ay = tilt - sides - axial
    az = -tilt - sides - axial
    even = 8.0 * k_e + k_eps
    both = k_pxx + k_pixx
    lean = k_pww + k_piww
    exy = even + both + lean
    exz = even + both - lean
    eyz = even - 2.0 * both
    ux, uy, uz = 4.0 * k_qx, 4.0 * k_qy, 4.0 * k_qz
    xy_x, xy_y = k_qx + k_mx, k_qy - k_my
    xz_x, xz_z = k_qx - k_mx, k_qz + k_mz
    yz_y, yz_z = k_qy + k_my, k_qz - k_mz
    p, m = exy + k_pxy, exy - k_pxy
    add, sub = xy_x + xy_y, xy_x - xy_y
    change = [12.0 * k_eps - 30.0 * k_e, ax - ux, ax + ux, ay - uy, ay + uy, az - uz, az + uz]
    change += [p + add, p - add, m + sub, m - sub]
    p, m = exz + k_pxz, exz - k_pxz
    add, sub = xz_x + xz_z, xz_x - xz_z
    change += [p + add, p - add, m + sub, m - sub]
    p, m = eyz + k_pyz, eyz - k_pyz
    add, sub = yz_y + yz_z, yz_y - yz_z
    change += [p + add, p - add, m + sub, m - sub]
    return [jnp.where(fluid, f[i] - change[i], f[OPP[i]]) for i in range(Q)]


def turned(v, by):
    return pltpu.roll(v, by % 128, 1) if by % 128 else v


def swapped(v):
    return pltpu.roll(v, 4, 0)


def kernel(
    dims, slots_ref, near_ref, pop_ref, mask_ref, out_ref, found, source_of, found_sem, *rest
):
    field, ext, side, stage_e, stage_l, back_e, back_l = rest[:7]
    rest = rest[7:]
    nx, nz, nc = dims
    nd = lax.axis_size("depth")
    per_x = nz * nc * CAP
    layer = lax.axis_index("depth")
    me = lax.axis_index("plane")
    core = me % nc
    z = (me // nc) % nz
    x = me // (nc * nz)
    mine = (z * nc + core) * CAP
    first_slot = me * CAP

    def plane(xx, zz, cc):
        return {"plane": (xx * nz + zz) * nc + cc}

    above = {"depth": (layer + 1) % nd}
    below = {"depth": (layer + nd - 1) % nd}
    ring = [plane(x, (z + far + nz) % nz, core) for far in (-1, 1, -2, 2)]
    twin = plane(x, z, 1 - core)
    across = [plane((x + k) % nx, z, core) for k in range(1, nx)]

    barrier = pltpu.get_barrier_semaphore()
    partners = [above, below, twin] + ring + across
    for other in partners:
        pl.semaphore_signal(barrier, inc=1, device_id=other, device_id_type=MESH)

    send_sems, recv_sems = rest[-2:]
    per_step = rest[:-2]
    used = [0]

    def copy(src, dst, device):
        n = used[0]
        used[0] += 1
        return pltpu.make_async_remote_copy(
            src_ref=src,
            dst_ref=dst,
            send_sem=send_sems.at[n],
            recv_sem=recv_sems.at[n],
            device_id=device,
            device_id_type=MESH,
        )

    lane = lax.broadcasted_iota(jnp.int32, (8, 128), 1)
    tile_row = lax.broadcasted_iota(jnp.int32, (8, 128), 0)
    zin, group = lane % BE, lane // BE
    low_half = tile_row < CAP

    def collide_all(step, up, down):
        for k in range(5):
            up[k] = jnp.zeros((8, 128), F32)
            down[k] = jnp.zeros((8, 128), F32)

        def body(n, carry):
            pair = pl.ds(2 * n, 2)
            if step == 0:
                f = [pop_ref[i, pair] * WEIGHTS[i] for i in range(Q)]
            else:
                f = [field[i, pair] for i in range(Q)]
            post = collided(f, mask_ref[pair] == 1)
            for i in range(Q):
                ext[i, pl.ds(2 * n + 1, 2)] = post[i]
            for j in range(2):
                at = 2 * n + j
                mine = zin == at
                for k, i in enumerate(ZPLUS):
                    moved = pltpu.roll(post[i][j], (at + 113) % 128, 1)
                    up[k] = jnp.where(mine, moved, up[k])
                for k, i in enumerate(ZMINUS):
                    down[k] = jnp.where(mine, pltpu.roll(post[i][j], at, 1), down[k])
            return carry

        lax.fori_loop(0, BE // 2, body, 0)

    def face_x(i):
        return ext[i, BE] if DIRS[i][0] > 0 else ext[i, 1]

    def face_y(i):
        upper = DIRS[i][1] > 0
        halves = []
        for q in range(2):
            part = None
            for k in range(8):
                moved = turned(ext[i, 1 + 8 * q + k], 16 * k + 16 * upper)
                part = moved if part is None else jnp.where(group == k, moved, part)
            halves.append(part)
        if upper:
            return jnp.where(low_half, swapped(halves[0]), halves[1])
        return jnp.where(low_half, halves[0], swapped(halves[1]))

    def by_slot(stage, faces, table):
        for s in range(CAP):
            for f in range(faces):
                table[mine + s, f] = stage[f, pl.ds(s, 8, stride=CAP), :]

    def pack_early(table):
        for f, dirs in enumerate(EARLY):
            for k, i in enumerate(dirs):
                stage_e[f, 8 * k : 8 * k + 8, :] = face_x(i) if f < 2 else face_y(i)
        stage_e[0, 24:32, :] = jnp.where(low_half, swapped(face_x(7)), swapped(face_x(9)))
        stage_e[1, 24:32, :] = jnp.where(low_half, swapped(face_x(10)), swapped(face_x(8)))
        for f in (2, 3):
            stage_e[f, 24:32, :] = jnp.zeros((8, 128), F32)
        by_slot(stage_e, 4, table)

    def shift_z(from_below, from_above, table):
        def body(at, carry):
            for k, i in enumerate(ZPLUS):
                rim = pltpu.roll(from_below[k], (128 - at) % 128, 1)
                ext[i, at + 1] = jnp.where(zin == 0, rim, pltpu.roll(ext[i, at + 1], 1, 1))
            for k, i in enumerate(ZMINUS):
                rim = pltpu.roll(from_above[k], 15 - at, 1)
                ext[i, at + 1] = jnp.where(
                    zin == BE - 1, rim, pltpu.roll(ext[i, at + 1], 127, 1)
                )
            return carry

        lax.fori_loop(0, BE, body, 0)
        for f, dirs in enumerate(LATE):
            for k, i in enumerate(dirs):
                stage_l[f, 8 * k : 8 * k + 8, :] = face_x(i) if f == 0 else face_y(i)
        by_slot(stage_l, 2, table)

    class Gather:
        def __init__(self, table):
            def block(far, first=0, count=CAP):
                start = (((z + far + 2 * nz) % nz) * nc + core) * CAP + first
                return table.at[pl.ds(start, count)]

            def send(far, to, first=0, count=CAP):
                part = block(far, first, count)
                return copy(part, part, plane(x, (z + to + nz) % nz, core))

            def to_twin(far):
                return copy(block(far), block(far), twin)

            self.two = [send(0, -2), send(0, 2)]
            self.one = [send(0, -1), send(0, 1)]
            self.own = to_twin(0)
            self.three = [send(2, -1), send(-2, 1)]
            self.four = [send(2, -2, 0, CAP // 2), send(-2, 2, CAP // 2, CAP // 2)]
            self.twin_one = [to_twin(1), to_twin(-1)]
            self.twin_two = [to_twin(2), to_twin(-2)]
            self.twin_three = [to_twin(3), to_twin(-3)]
            self.twin_four = to_twin(4)

        def begin(self):
            for c in self.two + self.one + [self.own]:
                c.start()

        def forward(self):
            for side in range(2):
                self.two[side].wait_recv()
                self.three[side].start()
                self.four[side].start()
                self.twin_two[side].start()
            for side in range(2):
                self.one[side].wait_recv()
                self.twin_one[side].start()

        def finish(self):
            for side in range(2):
                self.three[side].wait_recv()
                self.twin_three[side].start()
            for side in range(2):
                self.four[side].wait_recv()
            self.twin_four.start()
            for c in self.twin_all():
                c.wait_recv()

        def twin_all(self):
            return [self.own, *self.twin_one, *self.twin_two, *self.twin_three, self.twin_four]

        def sent(self):
            for c in self.two + self.one + self.three + self.four + self.twin_all():
                c.wait_send()

    def source(k, xx, s):
        return source_of[k, xx * per_x + mine + s]

    def early_row(table, to, base, xx):
        def body(s, carry):
            at = [source(k, xx, s) % per_x for k in range(8)]
            for tile, (main, six, seven) in enumerate(((0, 4, 6), (1, 7, 5))):
                got = jnp.where(tile_row == 6, table[at[six], tile], table[at[main], tile])
                to[base + s, tile] = jnp.where(tile_row == 7, table[at[seven], tile], got)
            to[base + s, 2] = table[at[2], 2]
            to[base + s, 3] = table[at[3], 3]
            return carry

        lax.fori_loop(0, CAP, body, 0)

    def late_row(table, to, base, xx):
        def body(s, carry):
            at = [source(k, xx, s) % per_x for k in range(4)]
            for tile in range(2):
                to[base + s, tile] = jnp.where(
                    tile_row < 4, table[at[2 * tile], tile], table[at[2 * tile + 1], tile]
                )
            return carry

        lax.fori_loop(0, CAP, body, 0)

    def hand_out(fill, table, out, got):
        sends = []
        for k in range(1, nx):
            fill(table, out, (k - 1) * CAP, (x + k) % nx)
            c = copy(
                out.at[pl.ds((k - 1) * CAP, CAP)], got.at[pl.ds(x * CAP, CAP)], across[k - 1]
            )
            c.start()
            sends.append(c)
        fill(table, got, x * CAP, x)
        return sends

    def place_halos(early, late):
        for s in range(CAP):
            of = [(source(k, x, s) // per_x) * CAP + s for k in range(8)]
            spread = pl.ds(s, 8, stride=CAP)
            for f, (main, six, seven) in enumerate(((0, 4, 6), (1, 7, 5))):
                got = jnp.where(tile_row == 6, early[of[six], f], early[of[main], f])
                back_e[f, spread, :] = jnp.where(tile_row == 7, early[of[seven], f], got)
            back_e[2, spread, :] = early[of[2], 2]
            back_e[3, spread, :] = early[of[3], 3]
            for f in range(2):
                back_l[f, spread, :] = jnp.where(
                    tile_row < 4, late[of[2 * f], f], late[of[2 * f + 1], f]
                )

        def put_x(i, tile):
            ext[i, 0 if DIRS[i][0] > 0 else BE + 1] = tile

        y_tiles = {}
        for f, dirs in enumerate(EARLY):
            for k, i in enumerate(dirs):
                tile = back_e[f, 8 * k : 8 * k + 8, :]
                if f < 2:
                    put_x(i, tile)
                else:
                    y_tiles[i] = tile
        for k, i in enumerate(LATE[0]):
            put_x(i, back_l[0, 8 * k : 8 * k + 8, :])
        for k, i in enumerate(LATE[1]):
            y_tiles[i] = back_l[1, 8 * k : 8 * k + 8, :]
        for f, ends in enumerate(((7, 9), (10, 8))):
            for i in ends:
                side[YDIRS.index(i), 0 if f == 0 else BE + 1] = back_e[f, 24:32, :]
        for j, i in enumerate(YDIRS):
            upper = DIRS[i][1] > 0
            tile = y_tiles[i]
            other = swapped(tile)
            for at in range(BE):
                part = tile if (at < 8) == upper else other
                side[j, at + 1] = turned(part, (112 if upper else 0) - 16 * (at % 8))

    def shift_xy(last):
        if last:
            held = jnp.zeros((8, 128), jnp.int32)
            for s in range(CAP):
                held = jnp.where(tile_row % CAP == s, source_of[8, first_slot + s], held)

        def body(at, carry):
            for i in range(Q):
                cx, cy, _ = DIRS[i]
                part = ext[i, at + 1 - cx]
                if cy:
                    beside = side[YDIRS.index(i), at + 1 - cx]
                    if cy > 0:
                        beside = jnp.where(low_half, beside, swapped(part))
                        part = pltpu.roll(jnp.where(group == 7, beside, part), BE, 1)
                    else:
                        beside = jnp.where(low_half, swapped(part), beside)
                        part = pltpu.roll(jnp.where(group == 0, beside, part), 128 - BE, 1)
                if last:
                    out_ref[i, at] = jnp.where(held == 1, part * (1.0 / WEIGHTS[i]), 0.0)
                else:
                    field[i, at] = part
            return carry

        lax.fori_loop(0, BE, body, 0)

    for step in range(STEPS):
        up, down, low, high, table_e, table_l, out_e, out_l, got_e, got_l = per_step[
            10 * step : 10 * step + 10
        ]
        collide_all(step, up, down)
        if step == 0:
            pl.semaphore_wait(barrier, len(partners))
        rims = [copy(up, low, above), copy(down, high, below)]
        for c in rims:
            c.start()
        pack_early(table_e)
        early = Gather(table_e)
        early.begin()
        if step == 0:
            find_sources(slots_ref, near_ref, found)
            to_scalars = pltpu.make_async_copy(found, source_of, found_sem)
            to_scalars.start()
            to_scalars.wait()
        for c in rims:
            c.wait_recv()
        shift_z(low, high, table_l)
        late = Gather(table_l)
        late.begin()
        early.forward()
        late.forward()
        early.finish()
        sends = hand_out(early_row, table_e, out_e, got_e)
        late.finish()
        sends += hand_out(late_row, table_l, out_l, got_l)
        for c in sends:
            c.wait_recv()
        place_halos(got_e, got_l)
        shift_xy(step == STEPS - 1)
        early.sent()
        late.sent()
        for c in rims + sends:
            c.wait_send()


def solution(mesh):
    planes = mesh.shape["plane"]
    dims = PLANE_DIMS[planes]
    nx, nz, nc = dims
    group = nz * nc * CAP

    def shards(populations, fluid_mask, block_per_slot, neighbours):
        slots = block_per_slot.shape[0]
        pops = populations[0].reshape(CAP, Q, BE, 2, 128).transpose(1, 2, 3, 0, 4)
        mask = fluid_mask[0].reshape(CAP, BE, 2, 128).transpose(1, 2, 0, 3)
        scratch = [
            pltpu.VMEM((16, slots), jnp.int32),
            pltpu.SMEM((16, slots), jnp.int32),
            pltpu.SemaphoreType.DMA,
            pltpu.VMEM((Q, BE, 8, 128), F32),
            pltpu.VMEM((Q, BE + 2, 8, 128), F32),
            pltpu.VMEM((len(YDIRS), BE + 2, 8, 128), F32),
            pltpu.VMEM((4, 32, 128), F32),
            pltpu.VMEM((2, 32, 128), F32),
            pltpu.VMEM((4, 32, 128), F32),
            pltpu.VMEM((2, 32, 128), F32),
        ]
        for _ in range(STEPS):
            scratch += [pltpu.VMEM((5, 8, 128), F32)] * 4
            for count, tiles in ((group, 4), (group, 2)):
                scratch.append(pltpu.VMEM((count, tiles, 8, 128), F32))
            for tiles in (4, 2):
                scratch.append(pltpu.VMEM(((nx - 1) * CAP, tiles, 8, 128), F32))
            for tiles in (4, 2):
                scratch.append(pltpu.VMEM((nx * CAP, tiles, 8, 128), F32))
        copies = STEPS * (2 + 2 * 16 + 2 * (nx - 1))
        scratch += [pltpu.SemaphoreType.DMA((copies,)), pltpu.SemaphoreType.DMA((copies,))]
        vmem = pl.BlockSpec(memory_space=pltpu.VMEM)
        out = pl.pallas_call(
            functools.partial(kernel, dims),
            out_shape=jax.ShapeDtypeStruct((Q, BE, 8, 128), F32),
            in_specs=[vmem] * 4,
            out_specs=vmem,
            scratch_shapes=scratch,
            compiler_params=pltpu.CompilerParams(
                collective_id=0, has_side_effects=True, vmem_limit_bytes=40 * 1024 * 1024
            ),
        )(
            block_per_slot.reshape(1, slots),
            neighbours.T,
            pops.reshape(Q, BE, 8, 128),
            mask.reshape(BE, 8, 128),
        )
        out = out.reshape(Q, BE, 2, CAP, 128).transpose(3, 0, 1, 2, 4)
        return out.reshape(populations.shape)

    return jax.shard_map(
        shards,
        mesh=mesh,
        in_specs=(P("depth", "plane", None, None), P("depth", "plane", None), P(), P()),
        out_specs=P("depth", "plane", None, None),
        check_vma=False,
    )
```

```python
import functools

import jax
import jax.numpy as jnp
from jax import lax
from jax.experimental import pallas as pl
from jax.experimental.pallas import tpu as pltpu
from jax.sharding import PartitionSpec as P

MESH = pl.DeviceIdType.MESH
BE = 16
CAP = 4
STEPS = 2
Q = 19
F32 = jnp.float32
PLANE_DIMS = {64: (4, 8, 2)}

DIRS = [
    (0, 0, 0),
    (1, 0, 0),
    (-1, 0, 0),
    (0, 1, 0),
    (0, -1, 0),
    (0, 0, 1),
    (0, 0, -1),
    (1, 1, 0),
    (-1, -1, 0),
    (1, -1, 0),
    (-1, 1, 0),
    (1, 0, 1),
    (-1, 0, -1),
    (1, 0, -1),
    (-1, 0, 1),
    (0, 1, 1),
    (0, -1, -1),
    (0, 1, -1),
    (0, -1, 1),
]
OPP = [0, 2, 1, 4, 3, 6, 5, 8, 7, 10, 9, 12, 11, 14, 13, 16, 15, 18, 17]
WEIGHTS = [1.0 / 3.0] + [1.0 / 18.0] * 6 + [1.0 / 36.0] * 12
ZPLUS = [5, 11, 14, 15, 18]
ZMINUS = [6, 12, 13, 16, 17]
CHUNKS = (((1, 7, 9), (2, 8, 10)), ((3, 7, 10), (4, 8, 9)), ((11, 13, 12, 14), (15, 17, 16, 18)))
YDIRS = [i for i in range(Q) if DIRS[i][1] != 0]


def top_rows(v):
    total = v[0:8]
    for r in range(8, v.shape[0], 8):
        total = jnp.maximum(total, v[r : r + 8])
    for t in (4, 2, 1):
        total = jnp.maximum(total, pltpu.roll(total, t, 0))
    return total


def find_sources(slots_ref, near_ref, out_ref):
    blocks, slots = near_ref.shape[1], slots_ref.shape[1]
    held = slots_ref[...]
    down = lax.broadcasted_iota(jnp.int32, (blocks, 128), 0)
    across = lax.broadcasted_iota(jnp.int32, (blocks, 128), 1)

    def upright(line):
        return jnp.transpose(jnp.broadcast_to(line, (128, 128)))

    lookup = jnp.zeros((8, 128), jnp.int32)
    for q in range(slots // 128):
        mine = upright(held[:, 128 * q : 128 * q + 128])
        lookup = jnp.maximum(lookup, top_rows(jnp.where(mine == across, down + 128 * q, 0)))

    def through(k, column):
        hit = jnp.broadcast_to(near_ref[k : k + 1, :], (blocks, 128)) == down
        return top_rows(jnp.where(hit, column, 0))[0:1]

    column = upright(lookup[0:1])
    found = [upright(through(k, column)) for k in range(4)]
    found += [upright(through(k, found[j])) for k, j in ((0, 2), (1, 3), (0, 3), (1, 2))]
    for q in range(slots // 128):
        part = slice(128 * q, 128 * q + 128)
        hit = jnp.broadcast_to(held[:, part], (blocks, 128)) == down
        for k in range(8):
            out_ref[k : k + 1, part] = top_rows(jnp.where(hit, found[k], 0))[0:1]
        out_ref[8:16, part] = jnp.broadcast_to(
            jnp.where(held[:, part] < blocks, 1, 0), (8, 128)
        )


def collided(f, fluid):
    s1, d1 = f[1] + f[2], f[1] - f[2]
    s2, d2 = f[3] + f[4], f[3] - f[4]
    s3, d3 = f[5] + f[6], f[5] - f[6]
    a, da = f[7] + f[8], f[7] - f[8]
    b, db = f[9] + f[10], f[9] - f[10]
    c, dc = f[11] + f[12], f[11] - f[12]
    d, dd = f[13] + f[14], f[13] - f[14]
    e, de = f[15] + f[16], f[15] - f[16]
    g, dg = f[17] + f[18], f[17] - f[18]
    sxy, sxz, syz = a + b, c + d, e + g
    x_xy, y_xy = da + db, da - db
    x_xz, z_xz = dc + dd, dc - dd
    y_yz, z_yz = de + dg, de - dg
    axis = s1 + s2 + s3
    diag = sxy + sxz + syz
    xx, yy, zz = x_xy + x_xz, y_xy + y_yz, z_xz + z_yz
    rho = f[0] + axis + diag
    jx, jy, jz = d1 + xx, d2 + yy, d3 + zz
    jx2, jy2, jz2 = jx * jx, jy * jy, jz * jz
    jsq = jx2 + jy2 + jz2
    pxx_eq = 2.0 * jx2 - jy2 - jz2
    pww_eq = jy2 - jz2
    m_e = 8.0 * diag - 11.0 * axis - 30.0 * f[0]
    m_eps = diag - 4.0 * axis + 12.0 * f[0]
    yz_axis = s2 + s3
    part = sxy + sxz - 2.0 * syz
    split = sxy - sxz
    turn = s2 - s3
    k_e = (1.19 / 2394.0) * (m_e + 11.0 * rho - 19.0 * jsq)
    k_eps = (1.4 / 252.0) * (m_eps - 3.0 * rho + 5.5 * jsq)
    k_qx = (1.2 / 40.0) * (xx - 4.0 * d1 + (2.0 / 3.0) * jx)
    k_qy = (1.2 / 40.0) * (yy - 4.0 * d2 + (2.0 / 3.0) * jy)
    k_qz = (1.2 / 40.0) * (zz - 4.0 * d3 + (2.0 / 3.0) * jz)
    k_pxx = (1.25 / 36.0) * (2.0 * s1 - yz_axis + part - pxx_eq)
    k_pixx = (1.4 / 72.0) * (2.0 * yz_axis - 4.0 * s1 + part + 0.5 * pxx_eq)
    k_pww = (1.25 / 12.0) * (turn + split - pww_eq)
    k_piww = (1.4 / 24.0) * (split - 2.0 * turn + 0.5 * pww_eq)
    k_pxy = (1.25 / 4.0) * (a - b - jx * jy)
    k_pyz = (1.25 / 4.0) * (e - g - jy * jz)
    k_pxz = (1.25 / 4.0) * (c - d - jx * jz)
    k_mx = (1.98 / 8.0) * (x_xy - x_xz)
    k_my = (1.98 / 8.0) * (y_yz - y_xy)
    k_mz = (1.98 / 8.0) * (z_xz - z_yz)
    axial = 11.0 * k_e + 4.0 * k_eps
    sides = k_pxx - 2.0 * k_pixx
    tilt = k_pww - 2.0 * k_piww
    ax = 2.0 * sides - axial
    ay = tilt - sides - axial
    az = -tilt - sides - axial
    even = 8.0 * k_e + k_eps
    both = k_pxx + k_pixx
    lean = k_pww + k_piww
    exy = even + both + lean
    exz = even + both - lean
    eyz = even - 2.0 * both
    ux, uy, uz = 4.0 * k_qx, 4.0 * k_qy, 4.0 * k_qz
    xy_x, xy_y = k_qx + k_mx, k_qy - k_my
    xz_x, xz_z = k_qx - k_mx, k_qz + k_mz
    yz_y, yz_z = k_qy + k_my, k_qz - k_mz
    p, m = exy + k_pxy, exy - k_pxy
    add, sub = xy_x + xy_y, xy_x - xy_y
    change = [12.0 * k_eps - 30.0 * k_e, ax - ux, ax + ux, ay - uy, ay + uy, az - uz, az + uz]
    change += [p + add, p - add, m + sub, m - sub]
    p, m = exz + k_pxz, exz - k_pxz
    add, sub = xz_x + xz_z, xz_x - xz_z
    change += [p + add, p - add, m + sub, m - sub]
    p, m = eyz + k_pyz, eyz - k_pyz
    add, sub = yz_y + yz_z, yz_y - yz_z
    change += [p + add, p - add, m + sub, m - sub]
    return [jnp.where(fluid, f[i] - change[i], f[OPP[i]]) for i in range(Q)]


def turned(v, by):
    return pltpu.roll(v, by % 128, 1) if by % 128 else v


def swapped(v):
    return pltpu.roll(v, 4, 0)


def kernel(
    dims, slots_in, near_in, pop_in, mask_in, out_ref, found, source_of, found_sem, *rest
):
    slots_ref, near_ref, pop_ref, mask_ref, in_sems, ext_a, ext_b, side, stage, back = rest[:10]
    rest = rest[10:]
    nx, nz, nc = dims
    nd = lax.axis_size("depth")
    per_x = nz * nc * CAP
    layer = lax.axis_index("depth")
    me = lax.axis_index("plane")
    core = me % nc
    z = (me // nc) % nz
    x = me // (nc * nz)
    mine = (z * nc + core) * CAP
    first_slot = me * CAP

    def plane(xx, zz, cc):
        return {"plane": (xx * nz + zz) * nc + cc}

    above = {"depth": (layer + 1) % nd}
    below = {"depth": (layer + nd - 1) % nd}
    ring = [plane(x, (z + far + nz) % nz, core) for far in (-1, 1, -2, 2)]
    twin = plane(x, z, 1 - core)
    across = [plane((x + k) % nx, z, core) for k in range(1, nx)]

    barrier = pltpu.get_barrier_semaphore()
    partners = [above, below, twin] + ring + across
    for other in partners:
        pl.semaphore_signal(barrier, inc=1, device_id=other, device_id_type=MESH)

    arguments = [
        pltpu.make_async_copy(src, dst, in_sems.at[n])
        for n, (src, dst) in enumerate(
            (
                (slots_in, slots_ref),
                (near_in, near_ref),
                (mask_in, mask_ref),
                (pop_in, pop_ref),
            )
        )
    ]
    for c in arguments:
        c.start()

    send_sems, recv_sems = rest[-2:]
    per_step = rest[:-2]
    used = [0]

    def copy(src, dst, device):
        n = used[0]
        used[0] += 1
        return pltpu.make_async_remote_copy(
            src_ref=src,
            dst_ref=dst,
            send_sem=send_sems.at[n],
            recv_sem=recv_sems.at[n],
            device_id=device,
            device_id_type=MESH,
        )

    lane = lax.broadcasted_iota(jnp.int32, (8, 128), 1)
    tile_row = lax.broadcasted_iota(jnp.int32, (8, 128), 0)
    zin, group = lane % BE, lane // BE
    low_half = tile_row < CAP

    def streamed(ext, at):
        parts = []
        for i in range(Q):
            cx, cy, _ = DIRS[i]
            part = ext[i, at + 1 - cx]
            if cy:
                beside = side[YDIRS.index(i), at + 1 - cx]
                if cy > 0:
                    beside = jnp.where(low_half, beside, swapped(part))
                    part = pltpu.roll(jnp.where(group == 7, beside, part), BE, 1)
                else:
                    beside = jnp.where(low_half, swapped(part), beside)
                    part = pltpu.roll(jnp.where(group == 0, beside, part), 128 - BE, 1)
            parts.append(part)
        return parts

    def collide(at, old, into, up, down):
        if old is None:
            f = [pop_ref[i, at] * WEIGHTS[i] for i in range(Q)]
        else:
            f = streamed(old, at)
        post = collided(f, mask_ref[at] == 1)
        for i in range(Q):
            into[i, at + 1] = post[i]
        mine = zin == at
        for k, i in enumerate(ZPLUS):
            up[k] = jnp.where(mine, pltpu.roll(post[i], (at + 113) % 128, 1), up[k])
        for k, i in enumerate(ZMINUS):
            down[k] = jnp.where(mine, pltpu.roll(post[i], at, 1), down[k])

    def collide_ends(*to):
        up, down = to[-2:]
        for k in range(5):
            up[k] = jnp.zeros((8, 128), F32)
            down[k] = jnp.zeros((8, 128), F32)
        for at in (0, BE - 1):
            collide(at, *to)

    def collide_rest(*to):
        def body(n, carry):
            collide(n, *to)
            collide(BE - 1 - n, *to)
            return carry

        lax.fori_loop(1, BE // 2, body, 0)

    def face_x(ext, i):
        return ext[i, BE] if DIRS[i][0] > 0 else ext[i, 1]

    def face_y(ext, i):
        upper = DIRS[i][1] > 0
        halves = []
        for q in range(2):
            part = None
            for k in range(8):
                moved = turned(ext[i, 1 + 8 * q + k], 16 * k + 16 * upper)
                part = moved if part is None else jnp.where(group == k, moved, part)
            halves.append(part)
        if upper:
            return jnp.where(low_half, swapped(halves[0]), halves[1])
        return jnp.where(low_half, halves[0], swapped(halves[1]))

    def pack(chunk, ext, table):
        for f, dirs in enumerate(CHUNKS[chunk]):
            for k, i in enumerate(dirs):
                along_x = chunk == 0 or (chunk == 2 and f == 0)
                stage[chunk, f, 8 * k : 8 * k + 8, :] = (
                    face_x(ext, i) if along_x else face_y(ext, i)
                )
        if chunk == 0:
            for f, (i, j) in enumerate(((7, 9), (10, 8))):
                ends = jnp.where(low_half, swapped(face_x(ext, i)), swapped(face_x(ext, j)))
                stage[chunk, f, 24:32, :] = ends
        if chunk == 1:
            for f in range(2):
                stage[chunk, f, 24:32, :] = jnp.zeros((8, 128), F32)
        for s in range(CAP):
            for f in range(2):
                table[mine + s, f] = stage[chunk, f, pl.ds(s, 8, stride=CAP), :]

    def shift_z(ext, from_below, from_above):
        def body(at, carry):
            for k, i in enumerate(ZPLUS):
                rim = pltpu.roll(from_below[k], (128 - at) % 128, 1)
                ext[i, at + 1] = jnp.where(zin == 0, rim, pltpu.roll(ext[i, at + 1], 1, 1))
            for k, i in enumerate(ZMINUS):
                rim = pltpu.roll(from_above[k], 15 - at, 1)
                ext[i, at + 1] = jnp.where(
                    zin == BE - 1, rim, pltpu.roll(ext[i, at + 1], 127, 1)
                )
            return carry

        lax.fori_loop(0, BE, body, 0)

    class Gather:
        def __init__(self, table):
            def block(far, first=0, count=CAP):
                start = (((z + far + 2 * nz) % nz) * nc + core) * CAP + first
                return table.at[pl.ds(start, count)]

            def send(far, to, first=0, count=CAP):
                part = block(far, first, count)
                return copy(part, part, plane(x, (z + to + nz) % nz, core))

            def to_twin(far):
                return copy(block(far), block(far), twin)

            self.two = [send(0, -2), send(0, 2)]
            self.one = [send(0, -1), send(0, 1)]
            self.own = to_twin(0)
            self.three = [send(2, -1), send(-2, 1)]
            self.four = [send(2, -2, 0, CAP // 2), send(-2, 2, CAP // 2, CAP // 2)]
            self.twin_one = [to_twin(1), to_twin(-1)]
            self.twin_two = [to_twin(2), to_twin(-2)]
            self.twin_three = [to_twin(3), to_twin(-3)]
            self.twin_four = to_twin(4)

        def begin(self):
            for c in self.two + self.one + [self.own]:
                c.start()

        def forward(self):
            for side in range(2):
                self.two[side].wait_recv()
                self.three[side].start()
                self.four[side].start()
                self.twin_two[side].start()
            for side in range(2):
                self.one[side].wait_recv()
                self.twin_one[side].start()

        def pass_on(self):
            for side in range(2):
                self.three[side].wait_recv()
                self.twin_three[side].start()
            for side in range(2):
                self.four[side].wait_recv()
            self.twin_four.start()

        def finish(self):
            for c in self.twin_all():
                c.wait_recv()

        def twin_all(self):
            return [self.own, *self.twin_one, *self.twin_two, *self.twin_three, self.twin_four]

        def sent(self):
            for c in self.two + self.one + self.three + self.four + self.twin_all():
                c.wait_send()

    def source(k, xx, s):
        return source_of[k, xx * per_x + mine + s]

    def merged(chunk, f, read):
        if chunk == 0:
            main, six, seven = ((0, 4, 6), (1, 7, 5))[f]
            got = jnp.where(tile_row == 6, read(six, f), read(main, f))
            return jnp.where(tile_row == 7, read(seven, f), got)
        if chunk == 1:
            return read(2 + f, f)
        return jnp.where(tile_row < 4, read(2 * f, f), read(2 * f + 1, f))

    def choose(chunk, table, to, base, xx):
        def body(s, carry):
            for f in range(2):
                to[base + s, f] = merged(
                    chunk, f, lambda k, f: table[source(k, xx, s) % per_x, f]
                )
            return carry

        lax.fori_loop(0, CAP, body, 0)

    def hand_out(chunk, table, out, got):
        sends = []
        for k in range(1, nx):
            choose(chunk, table, out, (k - 1) * CAP, (x + k) % nx)
            c = copy(
                out.at[pl.ds((k - 1) * CAP, CAP)], got.at[pl.ds(x * CAP, CAP)], across[k - 1]
            )
            c.start()
            sends.append(c)
        choose(chunk, table, got, x * CAP, x)
        return sends

    def place_halos(chunk, ext, got):
        for s in range(CAP):
            for f in range(2):
                back[chunk, f, pl.ds(s, 8, stride=CAP), :] = merged(
                    chunk, f, lambda k, f: got[(source(k, x, s) // per_x) * CAP + s, f]
                )
        for f, dirs in enumerate(CHUNKS[chunk]):
            for k, i in enumerate(dirs):
                tile = back[chunk, f, 8 * k : 8 * k + 8, :]
                if chunk == 0 or (chunk == 2 and f == 0):
                    ext[i, 0 if DIRS[i][0] > 0 else BE + 1] = tile
                    continue
                upper = DIRS[i][1] > 0
                other = swapped(tile)
                for at in range(BE):
                    part = tile if (at < 8) == upper else other
                    side[YDIRS.index(i), at + 1] = turned(
                        part, (112 if upper else 0) - 16 * (at % 8)
                    )
        if chunk == 0:
            for f, ends in enumerate(((7, 9), (10, 8))):
                for i in ends:
                    side[YDIRS.index(i), 0 if f == 0 else BE + 1] = back[0, f, 24:32, :]

    def give_out(ext):
        held = jnp.zeros((8, 128), jnp.int32)
        for s in range(CAP):
            held = jnp.where(tile_row % CAP == s, source_of[8, first_slot + s], held)

        def body(at, carry):
            for i, part in enumerate(streamed(ext, at)):
                out_ref[i, at] = jnp.where(held == 1, part * (1.0 / WEIGHTS[i]), 0.0)
            return carry

        lax.fori_loop(0, BE, body, 0)

    for step in range(STEPS):
        up, down, low, high, *buffers = per_step[13 * step : 13 * step + 13]
        tables, outs, gots = buffers[0:3], buffers[3:6], buffers[6:9]
        old, ext = (ext_b, ext_a) if step % 2 == 0 else (ext_a, ext_b)
        first, second, third = [Gather(table) for table in tables]
        to = (None if step == 0 else old, ext, up, down)
        if step == 0:
            for c in arguments:
                c.wait()
        collide_ends(*to)
        if step == 0:
            collide_rest(*to)
            find_sources(slots_ref, near_ref, found)
            to_scalars = pltpu.make_async_copy(found, source_of, found_sem)
            to_scalars.start()
            to_scalars.wait()
            pl.semaphore_wait(barrier, len(partners))
        rims = [copy(up, low, above), copy(down, high, below)]
        if step == 0:
            for c in rims:
                c.start()
        pack(0, ext, tables[0])
        first.begin()
        if step > 0:
            collide_rest(*to)
            for c in rims:
                c.start()
        pack(1, ext, tables[1])
        second.begin()
        for c in rims:
            c.wait_recv()
        shift_z(ext, low, high)
        pack(2, ext, tables[2])
        third.begin()
        first.forward()
        second.forward()
        third.forward()
        first.pass_on()
        first.finish()
        sends = [hand_out(0, tables[0], outs[0], gots[0])]
        second.pass_on()
        second.finish()
        sends.append(hand_out(1, tables[1], outs[1], gots[1]))
        third.pass_on()
        third.finish()
        sends.append(hand_out(2, tables[2], outs[2], gots[2]))
        for chunk in range(3):
            for c in sends[chunk]:
                c.wait_recv()
            place_halos(chunk, ext, gots[chunk])
        if step == STEPS - 1:
            give_out(ext)
        for gather in (first, second, third):
            gather.sent()
        for c in rims + sum(sends, []):
            c.wait_send()


def solution(mesh):
    planes = mesh.shape["plane"]
    dims = PLANE_DIMS[planes]
    nx, nz, nc = dims
    group = nz * nc * CAP

    def shards(populations, fluid_mask, block_per_slot, neighbours):
        slots = block_per_slot.shape[0]
        pops = populations[0].reshape(CAP, Q, BE, 2, 128).transpose(1, 2, 3, 0, 4)
        mask = fluid_mask[0].reshape(CAP, BE, 2, 128).transpose(1, 2, 0, 3)
        scratch = [
            pltpu.VMEM((16, slots), jnp.int32),
            pltpu.SMEM((16, slots), jnp.int32),
            pltpu.SemaphoreType.DMA,
            pltpu.VMEM((1, slots), jnp.int32),
            pltpu.VMEM(neighbours.shape[::-1], jnp.int32),
            pltpu.VMEM((Q, BE, 8, 128), F32),
            pltpu.VMEM((BE, 8, 128), jnp.int32),
            pltpu.SemaphoreType.DMA((4,)),
            pltpu.VMEM((Q, BE + 2, 8, 128), F32),
            pltpu.VMEM((Q, BE + 2, 8, 128), F32),
            pltpu.VMEM((len(YDIRS), BE + 2, 8, 128), F32),
            pltpu.VMEM((3, 2, 32, 128), F32),
            pltpu.VMEM((3, 2, 32, 128), F32),
        ]
        for _ in range(STEPS):
            scratch += [pltpu.VMEM((5, 8, 128), F32)] * 4
            for count in (group, (nx - 1) * CAP, nx * CAP):
                scratch += [pltpu.VMEM((count, 2, 8, 128), F32)] * 3
        copies = STEPS * (2 + 3 * (16 + nx - 1))
        scratch += [pltpu.SemaphoreType.DMA((copies,)), pltpu.SemaphoreType.DMA((copies,))]
        vmem = pl.BlockSpec(memory_space=pltpu.VMEM)
        out = pl.pallas_call(
            functools.partial(kernel, dims),
            out_shape=jax.ShapeDtypeStruct((Q, BE, 8, 128), F32),
            in_specs=[pl.BlockSpec(memory_space=pltpu.HBM)] * 4,
            out_specs=vmem,
            scratch_shapes=scratch,
            compiler_params=pltpu.CompilerParams(
                collective_id=0, has_side_effects=True, vmem_limit_bytes=40 * 1024 * 1024
            ),
        )(
            *(
                pltpu.with_memory_space_constraint(a, pltpu.HBM)
                for a in (
                    block_per_slot.reshape(1, slots),
                    neighbours.T,
                    pops.reshape(Q, BE, 8, 128),
                    mask.reshape(BE, 8, 128),
                )
            )
        )
        out = out.reshape(Q, BE, 2, CAP, 128).transpose(3, 0, 1, 2, 4)
        return out.reshape(populations.shape)

    return jax.shard_map(
        shards,
        mesh=mesh,
        in_specs=(P("depth", "plane", None, None), P("depth", "plane", None), P(), P()),
        out_specs=P("depth", "plane", None, None),
        check_vma=False,
    )
```

```python
import functools

import jax
import jax.numpy as jnp
from jax import lax
from jax.experimental import pallas as pl
from jax.experimental.pallas import tpu as pltpu
from jax.sharding import PartitionSpec as P

MESH = pl.DeviceIdType.MESH
BE = 16
CAP = 4
STEPS = 2
Q = 19
F32 = jnp.float32
PLANE_DIMS = {64: (4, 8, 2)}

DIRS = [
    (0, 0, 0),
    (1, 0, 0),
    (-1, 0, 0),
    (0, 1, 0),
    (0, -1, 0),
    (0, 0, 1),
    (0, 0, -1),
    (1, 1, 0),
    (-1, -1, 0),
    (1, -1, 0),
    (-1, 1, 0),
    (1, 0, 1),
    (-1, 0, -1),
    (1, 0, -1),
    (-1, 0, 1),
    (0, 1, 1),
    (0, -1, -1),
    (0, 1, -1),
    (0, -1, 1),
]
OPP = [0, 2, 1, 4, 3, 6, 5, 8, 7, 10, 9, 12, 11, 14, 13, 16, 15, 18, 17]
WEIGHTS = [1.0 / 3.0] + [1.0 / 18.0] * 6 + [1.0 / 36.0] * 12
ZPLUS = [5, 11, 14, 15, 18]
ZMINUS = [6, 12, 13, 16, 17]
CHUNKS = (((1, 7, 9), (2, 8, 10)), ((3, 7, 10), (4, 8, 9)), ((11, 13, 12, 14), (15, 17, 16, 18)))
YDIRS = [i for i in range(Q) if DIRS[i][1] != 0]


def top_rows(v):
    total = v[0:8]
    for r in range(8, v.shape[0], 8):
        total = jnp.maximum(total, v[r : r + 8])
    for t in (4, 2, 1):
        total = jnp.maximum(total, pltpu.roll(total, t, 0))
    return total


def find_sources(slots_ref, near_ref, out_ref):
    blocks, slots = near_ref.shape[1], slots_ref.shape[1]
    held = slots_ref[...]
    down = lax.broadcasted_iota(jnp.int32, (blocks, 128), 0)
    across = lax.broadcasted_iota(jnp.int32, (blocks, 128), 1)

    def upright(line):
        return jnp.transpose(jnp.broadcast_to(line, (128, 128)))

    lookup = jnp.zeros((8, 128), jnp.int32)
    for q in range(slots // 128):
        mine = upright(held[:, 128 * q : 128 * q + 128])
        lookup = jnp.maximum(lookup, top_rows(jnp.where(mine == across, down + 128 * q, 0)))

    def through(k, column):
        hit = jnp.broadcast_to(near_ref[k : k + 1, :], (blocks, 128)) == down
        return top_rows(jnp.where(hit, column, 0))[0:1]

    column = upright(lookup[0:1])
    found = [upright(through(k, column)) for k in range(4)]
    found += [upright(through(k, found[j])) for k, j in ((0, 2), (1, 3), (0, 3), (1, 2))]
    for q in range(slots // 128):
        part = slice(128 * q, 128 * q + 128)
        hit = jnp.broadcast_to(held[:, part], (blocks, 128)) == down
        for k in range(8):
            out_ref[k : k + 1, part] = top_rows(jnp.where(hit, found[k], 0))[0:1]
        out_ref[16:24, part] = jnp.broadcast_to(
            jnp.where(held[:, part] < blocks, 1, 0), (8, 128)
        )


def collided(f, fluid):
    s1, d1 = f[1] + f[2], f[1] - f[2]
    s2, d2 = f[3] + f[4], f[3] - f[4]
    s3, d3 = f[5] + f[6], f[5] - f[6]
    a, da = f[7] + f[8], f[7] - f[8]
    b, db = f[9] + f[10], f[9] - f[10]
    c, dc = f[11] + f[12], f[11] - f[12]
    d, dd = f[13] + f[14], f[13] - f[14]
    e, de = f[15] + f[16], f[15] - f[16]
    g, dg = f[17] + f[18], f[17] - f[18]
    sxy, sxz, syz = a + b, c + d, e + g
    x_xy, y_xy = da + db, da - db
    x_xz, z_xz = dc + dd, dc - dd
    y_yz, z_yz = de + dg, de - dg
    axis = s1 + s2 + s3
    diag = sxy + sxz + syz
    xx, yy, zz = x_xy + x_xz, y_xy + y_yz, z_xz + z_yz
    rho = f[0] + axis + diag
    jx, jy, jz = d1 + xx, d2 + yy, d3 + zz
    jx2, jy2, jz2 = jx * jx, jy * jy, jz * jz
    jsq = jx2 + jy2 + jz2
    pxx_eq = 2.0 * jx2 - jy2 - jz2
    pww_eq = jy2 - jz2
    m_e = 8.0 * diag - 11.0 * axis - 30.0 * f[0]
    m_eps = diag - 4.0 * axis + 12.0 * f[0]
    yz_axis = s2 + s3
    part = sxy + sxz - 2.0 * syz
    split = sxy - sxz
    turn = s2 - s3
    k_e = (1.19 / 2394.0) * (m_e + 11.0 * rho - 19.0 * jsq)
    k_eps = (1.4 / 252.0) * (m_eps - 3.0 * rho + 5.5 * jsq)
    k_qx = (1.2 / 40.0) * (xx - 4.0 * d1 + (2.0 / 3.0) * jx)
    k_qy = (1.2 / 40.0) * (yy - 4.0 * d2 + (2.0 / 3.0) * jy)
    k_qz = (1.2 / 40.0) * (zz - 4.0 * d3 + (2.0 / 3.0) * jz)
    k_pxx = (1.25 / 36.0) * (2.0 * s1 - yz_axis + part - pxx_eq)
    k_pixx = (1.4 / 72.0) * (2.0 * yz_axis - 4.0 * s1 + part + 0.5 * pxx_eq)
    k_pww = (1.25 / 12.0) * (turn + split - pww_eq)
    k_piww = (1.4 / 24.0) * (split - 2.0 * turn + 0.5 * pww_eq)
    k_pxy = (1.25 / 4.0) * (a - b - jx * jy)
    k_pyz = (1.25 / 4.0) * (e - g - jy * jz)
    k_pxz = (1.25 / 4.0) * (c - d - jx * jz)
    k_mx = (1.98 / 8.0) * (x_xy - x_xz)
    k_my = (1.98 / 8.0) * (y_yz - y_xy)
    k_mz = (1.98 / 8.0) * (z_xz - z_yz)
    axial = 11.0 * k_e + 4.0 * k_eps
    sides = k_pxx - 2.0 * k_pixx
    tilt = k_pww - 2.0 * k_piww
    ax = 2.0 * sides - axial
    ay = tilt - sides - axial
    az = -tilt - sides - axial
    even = 8.0 * k_e + k_eps
    both = k_pxx + k_pixx
    lean = k_pww + k_piww
    exy = even + both + lean
    exz = even + both - lean
    eyz = even - 2.0 * both
    ux, uy, uz = 4.0 * k_qx, 4.0 * k_qy, 4.0 * k_qz
    xy_x, xy_y = k_qx + k_mx, k_qy - k_my
    xz_x, xz_z = k_qx - k_mx, k_qz + k_mz
    yz_y, yz_z = k_qy + k_my, k_qz - k_mz
    p, m = exy + k_pxy, exy - k_pxy
    add, sub = xy_x + xy_y, xy_x - xy_y
    change = [12.0 * k_eps - 30.0 * k_e, ax - ux, ax + ux, ay - uy, ay + uy, az - uz, az + uz]
    change += [p + add, p - add, m + sub, m - sub]
    p, m = exz + k_pxz, exz - k_pxz
    add, sub = xz_x + xz_z, xz_x - xz_z
    change += [p + add, p - add, m + sub, m - sub]
    p, m = eyz + k_pyz, eyz - k_pyz
    add, sub = yz_y + yz_z, yz_y - yz_z
    change += [p + add, p - add, m + sub, m - sub]
    return [jnp.where(fluid, f[i] - change[i], f[OPP[i]]) for i in range(Q)]


def turned(v, by):
    return pltpu.roll(v, by % 128, 1) if by % 128 else v


def swapped(v):
    return pltpu.roll(v, 4, 0)


def kernel(
    dims, slots_in, near_in, pop_in, mask_in, out_ref, found, source_of, found_sem, *rest
):
    slots_ref, near_ref, pop_ref, mask_ref, in_sems, ext_a, ext_b, side, stage, back = rest[:10]
    rest = rest[10:]
    nx, nz, nc = dims
    nd = lax.axis_size("depth")
    per_x = nz * nc * CAP
    layer = lax.axis_index("depth")
    me = lax.axis_index("plane")
    core = me % nc
    z = (me // nc) % nz
    x = me // (nc * nz)
    mine = (z * nc + core) * CAP
    home = (core * nz + 2) * CAP
    first_slot = me * CAP

    def plane(xx, zz, cc):
        return {"plane": (xx * nz + zz) * nc + cc}

    above = {"depth": (layer + 1) % nd}
    below = {"depth": (layer + nd - 1) % nd}
    ring = [plane(x, (z + far + nz) % nz, core) for far in (-1, 1, -2, 2)]
    other = plane(x, z, 1 - core)
    across = [plane((x + k) % nx, z, core) for k in range(1, nx)]

    barrier = pltpu.get_barrier_semaphore()
    partners = [above, below, other] + ring + across
    for partner in partners:
        pl.semaphore_signal(barrier, inc=1, device_id=partner, device_id_type=MESH)

    arguments = [
        pltpu.make_async_copy(src, dst, in_sems.at[n])
        for n, (src, dst) in enumerate(
            (
                (slots_in, slots_ref),
                (near_in, near_ref),
                (mask_in, mask_ref),
                (pop_in, pop_ref),
            )
        )
    ]
    for c in arguments:
        c.start()

    send_sems, recv_sems = rest[-2:]
    per_step = rest[:-2]
    used = [0]

    def copy(src, dst, device):
        n = used[0]
        used[0] += 1
        return pltpu.make_async_remote_copy(
            src_ref=src,
            dst_ref=dst,
            send_sem=send_sems.at[n],
            recv_sem=recv_sems.at[n],
            device_id=device,
            device_id_type=MESH,
        )

    lane = lax.broadcasted_iota(jnp.int32, (8, 128), 1)
    tile_row = lax.broadcasted_iota(jnp.int32, (8, 128), 0)
    zin, group = lane % BE, lane // BE
    low_half = tile_row < CAP

    def streamed(ext, at):
        parts = []
        for i in range(Q):
            cx, cy, _ = DIRS[i]
            part = ext[i, at + 1 - cx]
            if cy:
                beside = side[YDIRS.index(i), at + 1 - cx]
                if cy > 0:
                    beside = jnp.where(low_half, beside, swapped(part))
                    part = pltpu.roll(jnp.where(group == 7, beside, part), BE, 1)
                else:
                    beside = jnp.where(low_half, swapped(part), beside)
                    part = pltpu.roll(jnp.where(group == 0, beside, part), 128 - BE, 1)
            parts.append(part)
        return parts

    def collide(at, old, into, up, down):
        if old is None:
            f = [pop_ref[i, at] * WEIGHTS[i] for i in range(Q)]
        else:
            f = streamed(old, at)
        post = collided(f, mask_ref[at] == 1)
        for i in range(Q):
            into[i, at + 1] = post[i]
        mine = zin == at
        for k, i in enumerate(ZPLUS):
            up[k] = jnp.where(mine, pltpu.roll(post[i], (at + 113) % 128, 1), up[k])
        for k, i in enumerate(ZMINUS):
            down[k] = jnp.where(mine, pltpu.roll(post[i], at, 1), down[k])

    def collide_ends(*to):
        up, down = to[-2:]
        for k in range(5):
            up[k] = jnp.zeros((8, 128), F32)
            down[k] = jnp.zeros((8, 128), F32)
        for at in (0, BE - 1):
            collide(at, *to)

    def collide_rest(*to):
        def body(n, carry):
            collide(n, *to)
            collide(BE - 1 - n, *to)
            return carry

        lax.fori_loop(1, BE // 2, body, 0)

    def face_x(ext, i):
        return ext[i, BE] if DIRS[i][0] > 0 else ext[i, 1]

    def face_y(ext, i):
        upper = DIRS[i][1] > 0
        halves = []
        for q in range(2):
            part = None
            for k in range(8):
                moved = turned(ext[i, 1 + 8 * q + k], 16 * k + 16 * upper)
                part = moved if part is None else jnp.where(group == k, moved, part)
            halves.append(part)
        if upper:
            return jnp.where(low_half, swapped(halves[0]), halves[1])
        return jnp.where(low_half, halves[0], swapped(halves[1]))

    def pack(chunk, ext, table):
        for f, dirs in enumerate(CHUNKS[chunk]):
            for k, i in enumerate(dirs):
                along_x = chunk == 0 or (chunk == 2 and f == 0)
                stage[chunk, f, 8 * k : 8 * k + 8, :] = (
                    face_x(ext, i) if along_x else face_y(ext, i)
                )
        if chunk == 0:
            for f, (i, j) in enumerate(((7, 9), (10, 8))):
                ends = jnp.where(low_half, swapped(face_x(ext, i)), swapped(face_x(ext, j)))
                stage[chunk, f, 24:32, :] = ends
        if chunk == 1:
            for f in range(2):
                stage[chunk, f, 24:32, :] = jnp.zeros((8, 128), F32)
        for s in range(CAP):
            for f in range(2):
                table[home + s, f] = stage[chunk, f, pl.ds(s, 8, stride=CAP), :]

    def shift_z(ext, from_below, from_above):
        def body(at, carry):
            for k, i in enumerate(ZPLUS):
                rim = pltpu.roll(from_below[k], (128 - at) % 128, 1)
                ext[i, at + 1] = jnp.where(zin == 0, rim, pltpu.roll(ext[i, at + 1], 1, 1))
            for k, i in enumerate(ZMINUS):
                rim = pltpu.roll(from_above[k], 15 - at, 1)
                ext[i, at + 1] = jnp.where(
                    zin == BE - 1, rim, pltpu.roll(ext[i, at + 1], 127, 1)
                )
            return carry

        lax.fori_loop(0, BE, body, 0)

    class Gather:
        def __init__(self, table):
            def block(place, count=1):
                return table.at[pl.ds((core * nz + place) * CAP, count * CAP)]

            def send(far, to):
                there = plane(x, (z + to + nz) % nz, core)
                return copy(block((far + 2) % nz), block((far - to + 2) % nz), there)

            self.two = [send(0, -2), send(0, 2)]
            self.one = [send(0, -1), send(0, 1)]
            self.three = [send(2, -1), send(-2, 1)]
            way = 1 - 2 * core
            there = plane(x, (z - 2 * way + nz) % nz, core)
            self.four = copy(block(2 * way + 2), block(6), there)
            self.twin = [copy(block(0, 5), block(0, 5), other), copy(block(5, 3), block(5, 3), other)]

        def begin(self):
            for c in self.two + self.one:
                c.start()

        def forward(self):
            for side in range(2):
                self.two[side].wait_recv()
                self.three[side].start()
            self.four.start()
            for c in self.one:
                c.wait_recv()
            self.twin[0].start()

        def pass_on(self):
            for c in self.three:
                c.wait_recv()
            self.four.wait_recv()
            self.twin[1].start()

        def finish(self):
            for c in self.twin:
                c.wait_recv()

        def sent(self):
            for c in self.two + self.one + self.three + [self.four] + self.twin:
                c.wait_send()

    def x_of(k, s):
        return source_of[k, x * per_x + mine + s]

    def source(k, xx, s):
        return source_of[8 + k, xx * per_x + mine + s]

    def merged(chunk, f, read):
        if chunk == 0:
            main, six, seven = ((0, 4, 6), (1, 7, 5))[f]
            got = jnp.where(tile_row == 6, read(six, f), read(main, f))
            return jnp.where(tile_row == 7, read(seven, f), got)
        if chunk == 1:
            return read(2 + f, f)
        return jnp.where(tile_row < 4, read(2 * f, f), read(2 * f + 1, f))

    def choose(chunk, table, to, base, xx):
        def body(s, carry):
            for f in range(2):
                to[base + s, f] = merged(
                    chunk, f, lambda k, f: table[source(k, xx, s), f]
                )
            return carry

        lax.fori_loop(0, CAP, body, 0)

    def hand_out(chunk, table, out, got):
        sends = []
        for k in range(1, nx):
            choose(chunk, table, out, (k - 1) * CAP, (x + k) % nx)
            c = copy(
                out.at[pl.ds((k - 1) * CAP, CAP)], got.at[pl.ds(x * CAP, CAP)], across[k - 1]
            )
            c.start()
            sends.append(c)
        choose(chunk, table, got, x * CAP, x)
        return sends

    def place_halos(chunk, ext, got):
        for s in range(CAP):
            for f in range(2):
                back[chunk, f, pl.ds(s, 8, stride=CAP), :] = merged(
                    chunk, f, lambda k, f: got[x_of(k, s) * CAP + s, f]
                )
        for f, dirs in enumerate(CHUNKS[chunk]):
            for k, i in enumerate(dirs):
                tile = back[chunk, f, 8 * k : 8 * k + 8, :]
                if chunk == 0 or (chunk == 2 and f == 0):
                    ext[i, 0 if DIRS[i][0] > 0 else BE + 1] = tile
                    continue
                upper = DIRS[i][1] > 0
                flipped = swapped(tile)
                for at in range(BE):
                    part = tile if (at < 8) == upper else flipped
                    side[YDIRS.index(i), at + 1] = turned(
                        part, (112 if upper else 0) - 16 * (at % 8)
                    )
        if chunk == 0:
            for f, ends in enumerate(((7, 9), (10, 8))):
                for i in ends:
                    side[YDIRS.index(i), 0 if f == 0 else BE + 1] = back[0, f, 24:32, :]

    def give_out(ext):
        held = jnp.zeros((8, 128), jnp.int32)
        for s in range(CAP):
            held = jnp.where(tile_row % CAP == s, source_of[16, first_slot + s], held)

        def body(at, carry):
            for i, part in enumerate(streamed(ext, at)):
                out_ref[i, at] = jnp.where(held == 1, part * (1.0 / WEIGHTS[i]), 0.0)
            return carry

        lax.fori_loop(0, BE, body, 0)

    for step in range(STEPS):
        up, down, low, high, *buffers = per_step[13 * step : 13 * step + 13]
        tables, outs, gots = buffers[0:3], buffers[3:6], buffers[6:9]
        old, ext = (ext_b, ext_a) if step % 2 == 0 else (ext_a, ext_b)
        first, second, third = [Gather(table) for table in tables]
        to = (None if step == 0 else old, ext, up, down)
        if step == 0:
            for c in arguments:
                c.wait()
        collide_ends(*to)
        if step == 0:
            collide_rest(*to)
            find_sources(slots_ref, near_ref, found)
            slot = found[0:8, :]
            ring = slot % per_x // CAP
            place = ring % nc * nz + (ring // nc + nz + 2 - z) % nz
            found[0:8, :] = slot // per_x
            found[8:16, :] = place * CAP + slot % CAP
            to_scalars = pltpu.make_async_copy(found, source_of, found_sem)
            to_scalars.start()
            to_scalars.wait()
            pl.semaphore_wait(barrier, len(partners))
        rims = [copy(up, low, above), copy(down, high, below)]
        if step == 0:
            for c in rims:
                c.start()
        pack(0, ext, tables[0])
        first.begin()
        if step > 0:
            collide_rest(*to)
            for c in rims:
                c.start()
        pack(1, ext, tables[1])
        second.begin()
        for c in rims:
            c.wait_recv()
        shift_z(ext, low, high)
        pack(2, ext, tables[2])
        third.begin()
        first.forward()
        second.forward()
        third.forward()
        first.pass_on()
        first.finish()
        sends = [hand_out(0, tables[0], outs[0], gots[0])]
        second.pass_on()
        second.finish()
        sends.append(hand_out(1, tables[1], outs[1], gots[1]))
        third.pass_on()
        third.finish()
        sends.append(hand_out(2, tables[2], outs[2], gots[2]))
        for chunk in range(3):
            for c in sends[chunk]:
                c.wait_recv()
            place_halos(chunk, ext, gots[chunk])
        if step == STEPS - 1:
            give_out(ext)
        for gather in (first, second, third):
            gather.sent()
        for c in rims + sum(sends, []):
            c.wait_send()


def solution(mesh):
    planes = mesh.shape["plane"]
    dims = PLANE_DIMS[planes]
    nx, nz, nc = dims
    group = nz * nc * CAP

    def shards(populations, fluid_mask, block_per_slot, neighbours):
        slots = block_per_slot.shape[0]
        pops = populations[0].reshape(CAP, Q, BE, 2, 128).transpose(1, 2, 3, 0, 4)
        mask = fluid_mask[0].reshape(CAP, BE, 2, 128).transpose(1, 2, 0, 3)
        scratch = [
            pltpu.VMEM((24, slots), jnp.int32),
            pltpu.SMEM((24, slots), jnp.int32),
            pltpu.SemaphoreType.DMA,
            pltpu.VMEM((1, slots), jnp.int32),
            pltpu.VMEM(neighbours.shape[::-1], jnp.int32),
            pltpu.VMEM((Q, BE, 8, 128), F32),
            pltpu.VMEM((BE, 8, 128), jnp.int32),
            pltpu.SemaphoreType.DMA((4,)),
            pltpu.VMEM((Q, BE + 2, 8, 128), F32),
            pltpu.VMEM((Q, BE + 2, 8, 128), F32),
            pltpu.VMEM((len(YDIRS), BE + 2, 8, 128), F32),
            pltpu.VMEM((3, 2, 32, 128), F32),
            pltpu.VMEM((3, 2, 32, 128), F32),
        ]
        for _ in range(STEPS):
            scratch += [pltpu.VMEM((5, 8, 128), F32)] * 4
            for count in (group, (nx - 1) * CAP, nx * CAP):
                scratch += [pltpu.VMEM((count, 2, 8, 128), F32)] * 3
        copies = STEPS * (2 + 3 * (9 + nx - 1))
        scratch += [pltpu.SemaphoreType.DMA((copies,)), pltpu.SemaphoreType.DMA((copies,))]
        vmem = pl.BlockSpec(memory_space=pltpu.VMEM)
        out = pl.pallas_call(
            functools.partial(kernel, dims),
            out_shape=jax.ShapeDtypeStruct((Q, BE, 8, 128), F32),
            in_specs=[pl.BlockSpec(memory_space=pltpu.HBM)] * 4,
            out_specs=vmem,
            scratch_shapes=scratch,
            compiler_params=pltpu.CompilerParams(
                collective_id=0, has_side_effects=True, vmem_limit_bytes=40 * 1024 * 1024
            ),
        )(
            *(
                pltpu.with_memory_space_constraint(a, pltpu.HBM)
                for a in (
                    block_per_slot.reshape(1, slots),
                    neighbours.T,
                    pops.reshape(Q, BE, 8, 128),
                    mask.reshape(BE, 8, 128),
                )
            )
        )
        out = out.reshape(Q, BE, 2, CAP, 128).transpose(3, 0, 1, 2, 4)
        return out.reshape(populations.shape)

    return jax.shard_map(
        shards,
        mesh=mesh,
        in_specs=(P("depth", "plane", None, None), P("depth", "plane", None), P(), P()),
        out_specs=P("depth", "plane", None, None),
        check_vma=False,
    )
```

```python
import functools

import jax
import jax.numpy as jnp
from jax import lax
from jax.experimental import pallas as pl
from jax.experimental.pallas import tpu as pltpu
from jax.sharding import PartitionSpec as P

MESH = pl.DeviceIdType.MESH
BE = 16
CAP = 4
STEPS = 2
Q = 19
F32 = jnp.float32
PLANE_DIMS = {64: (4, 8, 2)}

DIRS = [
    (0, 0, 0),
    (1, 0, 0),
    (-1, 0, 0),
    (0, 1, 0),
    (0, -1, 0),
    (0, 0, 1),
    (0, 0, -1),
    (1, 1, 0),
    (-1, -1, 0),
    (1, -1, 0),
    (-1, 1, 0),
    (1, 0, 1),
    (-1, 0, -1),
    (1, 0, -1),
    (-1, 0, 1),
    (0, 1, 1),
    (0, -1, -1),
    (0, 1, -1),
    (0, -1, 1),
]
OPP = [0, 2, 1, 4, 3, 6, 5, 8, 7, 10, 9, 12, 11, 14, 13, 16, 15, 18, 17]
WEIGHTS = [1.0 / 3.0] + [1.0 / 18.0] * 6 + [1.0 / 36.0] * 12
ZPLUS = [5, 11, 14, 15, 18]
ZMINUS = [6, 12, 13, 16, 17]
CHUNKS = (((1, 7, 9), (2, 8, 10)), ((3, 7, 10), (4, 8, 9)), ((11, 13, 12, 14), (15, 17, 16, 18)))
YDIRS = [i for i in range(Q) if DIRS[i][1] != 0]


def top_rows(v):
    total = v[0:8]
    for r in range(8, v.shape[0], 8):
        total = jnp.maximum(total, v[r : r + 8])
    for t in (4, 2, 1):
        total = jnp.maximum(total, pltpu.roll(total, t, 0))
    return total


def find_sources(slots_ref, near_ref, out_ref):
    blocks, slots = near_ref.shape[1], slots_ref.shape[1]
    held = slots_ref[...]
    down = lax.broadcasted_iota(jnp.int32, (blocks, 128), 0)
    across = lax.broadcasted_iota(jnp.int32, (blocks, 128), 1)

    def upright(line):
        return jnp.transpose(jnp.broadcast_to(line, (128, 128)))

    lookup = jnp.zeros((8, 128), jnp.int32)
    for q in range(slots // 128):
        mine = upright(held[:, 128 * q : 128 * q + 128])
        lookup = jnp.maximum(lookup, top_rows(jnp.where(mine == across, down + 128 * q, 0)))

    def through(k, column):
        hit = jnp.broadcast_to(near_ref[k : k + 1, :], (blocks, 128)) == down
        return top_rows(jnp.where(hit, column, 0))[0:1]

    column = upright(lookup[0:1])
    found = [upright(through(k, column)) for k in range(4)]
    found += [upright(through(k, found[j])) for k, j in ((0, 2), (1, 3), (0, 3), (1, 2))]
    for q in range(slots // 128):
        part = slice(128 * q, 128 * q + 128)
        hit = jnp.broadcast_to(held[:, part], (blocks, 128)) == down
        for k in range(8):
            out_ref[k : k + 1, part] = top_rows(jnp.where(hit, found[k], 0))[0:1]
        out_ref[16:24, part] = jnp.broadcast_to(
            jnp.where(held[:, part] < blocks, 1, 0), (8, 128)
        )


def collided(f, fluid):
    s1, d1 = f[1] + f[2], f[1] - f[2]
    s2, d2 = f[3] + f[4], f[3] - f[4]
    s3, d3 = f[5] + f[6], f[5] - f[6]
    a, da = f[7] + f[8], f[7] - f[8]
    b, db = f[9] + f[10], f[9] - f[10]
    c, dc = f[11] + f[12], f[11] - f[12]
    d, dd = f[13] + f[14], f[13] - f[14]
    e, de = f[15] + f[16], f[15] - f[16]
    g, dg = f[17] + f[18], f[17] - f[18]
    sxy, sxz, syz = a + b, c + d, e + g
    x_xy, y_xy = da + db, da - db
    x_xz, z_xz = dc + dd, dc - dd
    y_yz, z_yz = de + dg, de - dg
    axis = s1 + s2 + s3
    diag = sxy + sxz + syz
    xx, yy, zz = x_xy + x_xz, y_xy + y_yz, z_xz + z_yz
    rho = f[0] + axis + diag
    jx, jy, jz = d1 + xx, d2 + yy, d3 + zz
    jx2, jy2, jz2 = jx * jx, jy * jy, jz * jz
    jsq = jx2 + jy2 + jz2
    pxx_eq = 2.0 * jx2 - jy2 - jz2
    pww_eq = jy2 - jz2
    m_e = 8.0 * diag - 11.0 * axis - 30.0 * f[0]
    m_eps = diag - 4.0 * axis + 12.0 * f[0]
    yz_axis = s2 + s3
    part = sxy + sxz - 2.0 * syz
    split = sxy - sxz
    turn = s2 - s3
    k_e = (1.19 / 2394.0) * (m_e + 11.0 * rho - 19.0 * jsq)
    k_eps = (1.4 / 252.0) * (m_eps - 3.0 * rho + 5.5 * jsq)
    k_qx = (1.2 / 40.0) * (xx - 4.0 * d1 + (2.0 / 3.0) * jx)
    k_qy = (1.2 / 40.0) * (yy - 4.0 * d2 + (2.0 / 3.0) * jy)
    k_qz = (1.2 / 40.0) * (zz - 4.0 * d3 + (2.0 / 3.0) * jz)
    k_pxx = (1.25 / 36.0) * (2.0 * s1 - yz_axis + part - pxx_eq)
    k_pixx = (1.4 / 72.0) * (2.0 * yz_axis - 4.0 * s1 + part + 0.5 * pxx_eq)
    k_pww = (1.25 / 12.0) * (turn + split - pww_eq)
    k_piww = (1.4 / 24.0) * (split - 2.0 * turn + 0.5 * pww_eq)
    k_pxy = (1.25 / 4.0) * (a - b - jx * jy)
    k_pyz = (1.25 / 4.0) * (e - g - jy * jz)
    k_pxz = (1.25 / 4.0) * (c - d - jx * jz)
    k_mx = (1.98 / 8.0) * (x_xy - x_xz)
    k_my = (1.98 / 8.0) * (y_yz - y_xy)
    k_mz = (1.98 / 8.0) * (z_xz - z_yz)
    axial = 11.0 * k_e + 4.0 * k_eps
    sides = k_pxx - 2.0 * k_pixx
    tilt = k_pww - 2.0 * k_piww
    ax = 2.0 * sides - axial
    ay = tilt - sides - axial
    az = -tilt - sides - axial
    even = 8.0 * k_e + k_eps
    both = k_pxx + k_pixx
    lean = k_pww + k_piww
    exy = even + both + lean
    exz = even + both - lean
    eyz = even - 2.0 * both
    ux, uy, uz = 4.0 * k_qx, 4.0 * k_qy, 4.0 * k_qz
    xy_x, xy_y = k_qx + k_mx, k_qy - k_my
    xz_x, xz_z = k_qx - k_mx, k_qz + k_mz
    yz_y, yz_z = k_qy + k_my, k_qz - k_mz
    p, m = exy + k_pxy, exy - k_pxy
    add, sub = xy_x + xy_y, xy_x - xy_y
    change = [12.0 * k_eps - 30.0 * k_e, ax - ux, ax + ux, ay - uy, ay + uy, az - uz, az + uz]
    change += [p + add, p - add, m + sub, m - sub]
    p, m = exz + k_pxz, exz - k_pxz
    add, sub = xz_x + xz_z, xz_x - xz_z
    change += [p + add, p - add, m + sub, m - sub]
    p, m = eyz + k_pyz, eyz - k_pyz
    add, sub = yz_y + yz_z, yz_y - yz_z
    change += [p + add, p - add, m + sub, m - sub]
    return [jnp.where(fluid, f[i] - change[i], f[OPP[i]]) for i in range(Q)]


def turned(v, by):
    return pltpu.roll(v, by % 128, 1) if by % 128 else v


def swapped(v):
    return pltpu.roll(v, 4, 0)


def kernel(
    dims, slots_in, near_in, pop_in, mask_in, out_ref, found, source_of, found_sem, *rest
):
    slots_ref, near_ref, pop_ref, mask_ref, in_sems, ext_a, ext_b, side, stage, back = rest[:10]
    rest = rest[10:]
    nx, nz, nc = dims
    nd = lax.axis_size("depth")
    per_x = nz * nc * CAP
    layer = lax.axis_index("depth")
    me = lax.axis_index("plane")
    core = me % nc
    z = (me // nc) % nz
    x = me // (nc * nz)
    mine = (z * nc + core) * CAP
    home = (core * nz + 2) * CAP
    first_slot = me * CAP

    def plane(xx, zz, cc):
        return {"plane": (xx * nz + zz) * nc + cc}

    above = {"depth": (layer + 1) % nd}
    below = {"depth": (layer + nd - 1) % nd}
    ring = [plane(x, (z + far + nz) % nz, core) for far in (-1, 1, -2, 2)]
    other = plane(x, z, 1 - core)
    across = [plane((x + k) % nx, z, core) for k in range(1, nx)]

    barrier = pltpu.get_barrier_semaphore()
    partners = [above, below, other] + ring + across
    for partner in partners:
        pl.semaphore_signal(barrier, inc=1, device_id=partner, device_id_type=MESH)

    arguments = [
        pltpu.make_async_copy(src, dst, in_sems.at[n])
        for n, (src, dst) in enumerate(
            (
                (slots_in, slots_ref),
                (near_in, near_ref),
                (mask_in, mask_ref),
                (pop_in, pop_ref),
            )
        )
    ]
    for c in arguments:
        c.start()

    send_sems, recv_sems = rest[-2:]
    per_step = rest[:-2]
    used = [0]

    def copy(src, dst, device):
        n = used[0]
        used[0] += 1
        return pltpu.make_async_remote_copy(
            src_ref=src,
            dst_ref=dst,
            send_sem=send_sems.at[n],
            recv_sem=recv_sems.at[n],
            device_id=device,
            device_id_type=MESH,
        )

    lane = lax.broadcasted_iota(jnp.int32, (8, 128), 1)
    tile_row = lax.broadcasted_iota(jnp.int32, (8, 128), 0)
    zin, group = lane % BE, lane // BE
    low_half = tile_row < CAP

    def streamed(ext, at):
        parts = []
        for i in range(Q):
            cx, cy, _ = DIRS[i]
            part = ext[i, at + 1 - cx]
            if cy:
                beside = side[YDIRS.index(i), at + 1 - cx]
                if cy > 0:
                    beside = jnp.where(low_half, beside, swapped(part))
                    part = pltpu.roll(jnp.where(group == 7, beside, part), BE, 1)
                else:
                    beside = jnp.where(low_half, swapped(part), beside)
                    part = pltpu.roll(jnp.where(group == 0, beside, part), 128 - BE, 1)
            parts.append(part)
        return parts

    def collide(at, old, into, up, down):
        if old is None:
            f = [pop_ref[i, at] * WEIGHTS[i] for i in range(Q)]
        else:
            f = streamed(old, at)
        post = collided(f, mask_ref[at] == 1)
        for i in range(Q):
            into[i, at + 1] = post[i]
        mine = zin == at
        for k, i in enumerate(ZPLUS):
            up[k] = jnp.where(mine, pltpu.roll(post[i], (at + 113) % 128, 1), up[k])
        for k, i in enumerate(ZMINUS):
            down[k] = jnp.where(mine, pltpu.roll(post[i], at, 1), down[k])

    def collide_ends(*to):
        up, down = to[-2:]
        for k in range(5):
            up[k] = jnp.zeros((8, 128), F32)
            down[k] = jnp.zeros((8, 128), F32)
        for at in (0, BE - 1):
            collide(at, *to)

    def collide_rest(*to):
        def body(n, carry):
            collide(n, *to)
            collide(BE - 1 - n, *to)
            return carry

        lax.fori_loop(1, BE // 2, body, 0)

    def face_x(ext, i):
        return ext[i, BE] if DIRS[i][0] > 0 else ext[i, 1]

    def face_y(ext, i):
        upper = DIRS[i][1] > 0
        halves = []
        for q in range(2):
            part = None
            for k in range(8):
                moved = turned(ext[i, 1 + 8 * q + k], 16 * k + 16 * upper)
                part = moved if part is None else jnp.where(group == k, moved, part)
            halves.append(part)
        if upper:
            return jnp.where(low_half, swapped(halves[0]), halves[1])
        return jnp.where(low_half, halves[0], swapped(halves[1]))

    def pack(chunk, ext, table):
        for f, dirs in enumerate(CHUNKS[chunk]):
            for k, i in enumerate(dirs):
                along_x = chunk == 0 or (chunk == 2 and f == 0)
                stage[chunk, f, 8 * k : 8 * k + 8, :] = (
                    face_x(ext, i) if along_x else face_y(ext, i)
                )
        if chunk == 0:
            for f, (i, j) in enumerate(((7, 9), (10, 8))):
                ends = jnp.where(low_half, swapped(face_x(ext, i)), swapped(face_x(ext, j)))
                stage[chunk, f, 24:32, :] = ends
        if chunk == 1:
            for f in range(2):
                stage[chunk, f, 24:32, :] = jnp.zeros((8, 128), F32)
        for s in range(CAP):
            for f in range(2):
                table[home + s, f] = stage[chunk, f, pl.ds(s, 8, stride=CAP), :]

    def shift_z(ext, from_below, from_above, dirs, start, stop):
        def body(at, carry):
            for i in dirs:
                part = ext[i, at + 1]
                if i in ZPLUS:
                    rim = pltpu.roll(from_below[ZPLUS.index(i)], (128 - at) % 128, 1)
                    ext[i, at + 1] = jnp.where(zin == 0, rim, pltpu.roll(part, 1, 1))
                else:
                    rim = pltpu.roll(from_above[ZMINUS.index(i)], 15 - at, 1)
                    ext[i, at + 1] = jnp.where(zin == BE - 1, rim, pltpu.roll(part, 127, 1))
            return carry

        lax.fori_loop(start, stop, body, 0)

    class Gather:
        def __init__(self, table):
            def block(place, count=1):
                return table.at[pl.ds((core * nz + place) * CAP, count * CAP)]

            def send(far, to):
                there = plane(x, (z + to + nz) % nz, core)
                return copy(block((far + 2) % nz), block((far - to + 2) % nz), there)

            self.two = [send(0, -2), send(0, 2)]
            self.one = [send(0, -1), send(0, 1)]
            self.three = [send(2, -1), send(-2, 1)]
            way = 1 - 2 * core
            there = plane(x, (z - 2 * way + nz) % nz, core)
            self.four = copy(block(2 * way + 2), block(6), there)
            self.twin = [copy(block(0, 5), block(0, 5), other), copy(block(5, 3), block(5, 3), other)]

        def begin(self):
            for c in self.two + self.one:
                c.start()

        def forward(self):
            for side in range(2):
                self.two[side].wait_recv()
                self.three[side].start()
            self.four.start()

        def pass_on(self):
            for c in self.one:
                c.wait_recv()
            self.twin[0].start()
            for c in self.three:
                c.wait_recv()
            self.four.wait_recv()
            self.twin[1].start()

        def finish(self):
            for c in self.twin:
                c.wait_recv()

        def sent(self):
            for c in self.two + self.one + self.three + [self.four] + self.twin:
                c.wait_send()

    def x_of(k, s):
        return source_of[k, x * per_x + mine + s]

    def source(k, xx, s):
        return source_of[8 + k, xx * per_x + mine + s]

    def merged(chunk, f, read):
        if chunk == 0:
            main, six, seven = ((0, 4, 6), (1, 7, 5))[f]
            got = jnp.where(tile_row == 6, read(six, f), read(main, f))
            return jnp.where(tile_row == 7, read(seven, f), got)
        if chunk == 1:
            return read(2 + f, f)
        return jnp.where(tile_row < 4, read(2 * f, f), read(2 * f + 1, f))

    def choose(chunk, table, to, base, xx):
        def body(s, carry):
            for f in range(2):
                to[base + s, f] = merged(
                    chunk, f, lambda k, f: table[source(k, xx, s), f]
                )
            return carry

        lax.fori_loop(0, CAP, body, 0)

    def hand_out(chunk, table, out, got):
        sends = []
        for k in range(1, nx):
            choose(chunk, table, out, (k - 1) * CAP, (x + k) % nx)
            c = copy(
                out.at[pl.ds((k - 1) * CAP, CAP)], got.at[pl.ds(x * CAP, CAP)], across[k - 1]
            )
            c.start()
            sends.append(c)
        choose(chunk, table, got, x * CAP, x)
        return sends

    def place_halos(chunk, ext, got):
        for s in range(CAP):
            for f in range(2):
                back[chunk, f, pl.ds(s, 8, stride=CAP), :] = merged(
                    chunk, f, lambda k, f: got[x_of(k, s) * CAP + s, f]
                )
        for f, dirs in enumerate(CHUNKS[chunk]):
            for k, i in enumerate(dirs):
                tile = back[chunk, f, 8 * k : 8 * k + 8, :]
                if chunk == 0 or (chunk == 2 and f == 0):
                    ext[i, 0 if DIRS[i][0] > 0 else BE + 1] = tile
                    continue
                upper = DIRS[i][1] > 0
                flipped = swapped(tile)
                for at in range(BE):
                    part = tile if (at < 8) == upper else flipped
                    side[YDIRS.index(i), at + 1] = turned(
                        part, (112 if upper else 0) - 16 * (at % 8)
                    )
        if chunk == 0:
            for f, ends in enumerate(((7, 9), (10, 8))):
                for i in ends:
                    side[YDIRS.index(i), 0 if f == 0 else BE + 1] = back[0, f, 24:32, :]

    def give_out(ext):
        held = jnp.zeros((8, 128), jnp.int32)
        for s in range(CAP):
            held = jnp.where(tile_row % CAP == s, source_of[16, first_slot + s], held)

        def body(at, carry):
            for i, part in enumerate(streamed(ext, at)):
                out_ref[i, at] = jnp.where(held == 1, part * (1.0 / WEIGHTS[i]), 0.0)
            return carry

        lax.fori_loop(0, BE, body, 0)

    for step in range(STEPS):
        up, down, low, high, *buffers = per_step[13 * step : 13 * step + 13]
        tables, outs, gots = buffers[0:3], buffers[3:6], buffers[6:9]
        old, ext = (ext_b, ext_a) if step % 2 == 0 else (ext_a, ext_b)
        first, second, third = [Gather(table) for table in tables]
        to = (None if step == 0 else old, ext, up, down)
        if step == 0:
            for c in arguments:
                c.wait()
        collide_ends(*to)
        if step == 0:
            collide_rest(*to)
            find_sources(slots_ref, near_ref, found)
            slot = found[0:8, :]
            ring = slot % per_x // CAP
            place = ring % nc * nz + (ring // nc + nz + 2 - z) % nz
            found[0:8, :] = slot // per_x
            found[8:16, :] = place * CAP + slot % CAP
            to_scalars = pltpu.make_async_copy(found, source_of, found_sem)
            to_scalars.start()
            to_scalars.wait()
            pl.semaphore_wait(barrier, len(partners))
        rims = [copy(up, low, above), copy(down, high, below)]
        if step == 0:
            for c in rims:
                c.start()
        pack(0, ext, tables[0])
        first.begin()
        if step > 0:
            collide_rest(*to)
            for c in rims:
                c.start()
        pack(1, ext, tables[1])
        second.begin()
        for c in rims:
            c.wait_recv()
        shift_z(ext, low, high, CHUNKS[2][1], 0, BE)
        shift_z(ext, low, high, CHUNKS[2][0], 0, 1)
        shift_z(ext, low, high, CHUNKS[2][0], BE - 1, BE)
        pack(2, ext, tables[2])
        third.begin()
        shift_z(ext, low, high, CHUNKS[2][0], 1, BE - 1)
        shift_z(ext, low, high, (5, 6), 0, BE)
        first.forward()
        second.forward()
        third.forward()
        first.pass_on()
        first.finish()
        sends = [hand_out(0, tables[0], outs[0], gots[0])]
        second.pass_on()
        second.finish()
        sends.append(hand_out(1, tables[1], outs[1], gots[1]))
        third.pass_on()
        third.finish()
        sends.append(hand_out(2, tables[2], outs[2], gots[2]))
        for chunk in range(3):
            for c in sends[chunk]:
                c.wait_recv()
            place_halos(chunk, ext, gots[chunk])
        if step == STEPS - 1:
            give_out(ext)
        for gather in (first, second, third):
            gather.sent()
        for c in rims + sum(sends, []):
            c.wait_send()


def solution(mesh):
    planes = mesh.shape["plane"]
    dims = PLANE_DIMS[planes]
    nx, nz, nc = dims
    group = nz * nc * CAP

    def shards(populations, fluid_mask, block_per_slot, neighbours):
        slots = block_per_slot.shape[0]
        pops = populations[0].reshape(CAP, Q, BE, 2, 128).transpose(1, 2, 3, 0, 4)
        mask = fluid_mask[0].reshape(CAP, BE, 2, 128).transpose(1, 2, 0, 3)
        scratch = [
            pltpu.VMEM((24, slots), jnp.int32),
            pltpu.SMEM((24, slots), jnp.int32),
            pltpu.SemaphoreType.DMA,
            pltpu.VMEM((1, slots), jnp.int32),
            pltpu.VMEM(neighbours.shape[::-1], jnp.int32),
            pltpu.VMEM((Q, BE, 8, 128), F32),
            pltpu.VMEM((BE, 8, 128), jnp.int32),
            pltpu.SemaphoreType.DMA((4,)),
            pltpu.VMEM((Q, BE + 2, 8, 128), F32),
            pltpu.VMEM((Q, BE + 2, 8, 128), F32),
            pltpu.VMEM((len(YDIRS), BE + 2, 8, 128), F32),
            pltpu.VMEM((3, 2, 32, 128), F32),
            pltpu.VMEM((3, 2, 32, 128), F32),
        ]
        for _ in range(STEPS):
            scratch += [pltpu.VMEM((5, 8, 128), F32)] * 4
            for count in (group, (nx - 1) * CAP, nx * CAP):
                scratch += [pltpu.VMEM((count, 2, 8, 128), F32)] * 3
        copies = STEPS * (2 + 3 * (9 + nx - 1))
        scratch += [pltpu.SemaphoreType.DMA((copies,)), pltpu.SemaphoreType.DMA((copies,))]
        vmem = pl.BlockSpec(memory_space=pltpu.VMEM)
        out = pl.pallas_call(
            functools.partial(kernel, dims),
            out_shape=jax.ShapeDtypeStruct((Q, BE, 8, 128), F32),
            in_specs=[pl.BlockSpec(memory_space=pltpu.HBM)] * 4,
            out_specs=vmem,
            scratch_shapes=scratch,
            compiler_params=pltpu.CompilerParams(
                collective_id=0, has_side_effects=True, vmem_limit_bytes=40 * 1024 * 1024
            ),
        )(
            *(
                pltpu.with_memory_space_constraint(a, pltpu.HBM)
                for a in (
                    block_per_slot.reshape(1, slots),
                    neighbours.T,
                    pops.reshape(Q, BE, 8, 128),
                    mask.reshape(BE, 8, 128),
                )
            )
        )
        out = out.reshape(Q, BE, 2, CAP, 128).transpose(3, 0, 1, 2, 4)
        return out.reshape(populations.shape)

    return jax.shard_map(
        shards,
        mesh=mesh,
        in_specs=(P("depth", "plane", None, None), P("depth", "plane", None), P(), P()),
        out_specs=P("depth", "plane", None, None),
        check_vma=False,
    )
```
